32 devices in a mesh: row: 4 (over z), col: 8 (over y, x, core).
Axes of the slice: x: 2, y: 2, z: 4, core: 2. Of those that a mesh axis runs over, the one named last changes fastest.
Arguments:
- a_panels: float32 [4096, 2048], P('row', 'col'), may hold values from -6 to 6
- b_panels: float32 [2048, 16384], P('row', 'col'), may hold values from -0.1875 to 0.1875
- a_occupancy: int32 [32, 16], P('row', 'col'), may hold values 0 or 1
- b_occupancy: int32 [16, 128], P('row', 'col'), may hold values 0 or 1
- owner_device: int32 [4, 8, 128, 1], P('row', 'col'), may hold values from 0 to 31; in each aligned block of 128 rows (0 to 127, 128 to 255, ..., all dimensions but the last counted through in order) at most 8 rows name the same one
- owner_block: int32 [4, 8, 128], P('row', 'col'), may hold values from 0 to 127
- c_previous: float32 [4, 8, 128, 128, 128], P('row', 'col'), may hold values from -6 to 6
Outputs:
- c_owned: float32 [4, 8, 128, 128, 128], P('row', 'col')
The draws below stay inside these ranges and needn't reach their ends.
Inputs may be any that keep to these rules, and one draw needn't show every extreme that they name: `owner_device`: among the 128 product blocks of one device, at most 8 name the same owner; some owner is named exactly 8 times by one device.
All inputs are finite; a program needn't handle non-finite values. No bound on the sum of `a_occupancy` or of `b_occupancy` on one device may be relied on, other than what follows from the above.
Results may differ from the reference program's by a relative error of at most 0.0003.
Values sent between devices are 32-bit elements; how exact they have to be, the bound alone decides.
No kernel may reach another device: no remote copies, remote signals or barrier semaphores. Data moves between devices by JAX's collectives and lax.ppermute only.
A program may use at most 192 MiB of HBM per device.

```python
import math
import jax
import jax.numpy as jnp
import numpy as np
from jax import lax

BLK = 128
P_SIZE = 8
Q = 16
K = 2
TICKS = 4
NBLK = 128
OWN = 128
IMAGES = 2
CAP = 8
N_ROW = 4
N_COL = 8


def touch_ends(drawn, stream_key, least, high):
    longest = drawn.shape.index(max(drawn.shape))
    spots = []
    for shift in (0, 1):
        where = [jax.random.randint(jax.random.fold_in(stream_key, axis), (), 0, length) for axis, length in enumerate(drawn.shape)]
        where[longest] = (where[longest] + shift) % drawn.shape[longest]
        spots.append(tuple(where))
    return drawn.at[spots[0]].set(least).at[spots[1]].set(high)


def steps_of(stream_key, extent, cuts, least, top_value):
    def one(position, parts):
        heights = jax.random.uniform(jax.random.fold_in(jax.random.fold_in(stream_key, 6), position), (parts,), jnp.float32, least / len(cuts), top_value / len(cuts))
        return jnp.repeat(jnp.exp(heights), extent[position] // parts).reshape((-1,) + (1,) * (len(extent) - position - 1))

    factor_of = one(*cuts[0])
    for cut in cuts[1:]:
        factor_of = factor_of * one(*cut)
    return factor_of


def shared_out(own_key, own, number, rows, count, top, reach, lean):
    order = jax.random.permutation(own_key, count)
    heavy_load, usual = shares(count, rows * top, reach, lean, True), shares(count, rows * top, reach, lean, False)
    places = jnp.arange(count)

    def named(sizes, turn):
        used = int((sizes > 0).sum())
        fixed = max(1, used // 4)
        passed = fixed + (places - fixed + turn * (used - fixed)) % max(1, count - fixed)
        return jnp.zeros((count,), jnp.int32).at[order[jnp.where(places < fixed, places, passed)]].set(jnp.asarray(sizes, jnp.int32))

    sizes = jnp.where(number % 4 == 0, named(heavy_load, number // 4), named(usual, number - number // 4 - 1))
    mixed = jax.random.permutation(jax.random.fold_in(own, 3), count)
    giver, sink = mixed[0:count // 2 * 2:2], mixed[1:count // 2 * 2:2]
    slack = jnp.minimum(sizes[giver] - 1, reach - sizes[sink]) // 2
    slack = jnp.where((giver == order[0]) | (sink == order[0]) | (sizes[sink] == 0), 0, jnp.maximum(slack, 0))
    passed = jax.random.randint(jax.random.fold_in(own, 4), (count // 2,), 0, 1 << 20) % (slack + 1)
    sizes = sizes.at[giver].add(-passed).at[sink].add(passed)
    items = jnp.searchsorted(jnp.cumsum(sizes), jnp.arange(rows * top), side="right").astype(jnp.int32)
    grid = items.reshape(top, rows).T
    grid = grid[jax.random.permutation(jax.random.fold_in(own, 1), rows)]
    turn = jax.random.randint(jax.random.fold_in(own, 2), (rows, 1), 0, top)
    return jnp.take_along_axis(grid, (jnp.arange(top)[None, :] + turn) % top, axis=1)


def shares(amount, total, limit, lean, full):
    loads = [(1 << 20) // math.isqrt(standing ** lean) + 1 for standing in range(1, amount + 1)]
    largest = limit if full else min(limit, max(-(-total // amount), total * loads[0] // sum(loads)))
    least = 1 if total - largest >= amount - 1 else 0
    holding, spare = [largest] + [least] * (amount - 1), total - largest - least * (amount - 1)
    while spare > 0:
        candidates = [i for i in range(1, amount) if holding[i] < largest] or [i for i in range(1, amount) if holding[i] < limit]
        whole, left = sum([loads[i] for i in candidates]), spare
        for i in candidates:
            extra = min(limit - holding[i], max(1, left * loads[i] // whole), spare)
            holding[i] = holding[i] + extra
            spare = spare - extra
    return np.array(holding)


def scatter_about(key, extent, scale, most, cuts=(), held_as=jnp.bfloat16):
    factor_of = steps_of(key, extent, cuts, -0.22, 0.18) if cuts else 1.0
    drawn = jax.random.normal(key, extent, jnp.float32) * scale * factor_of
    return jnp.minimum(jnp.maximum(drawn, -most), most).astype(held_as)


def setup_inputs(seed: int = 0) -> dict:
    streams_of = jax.random.split(jax.random.key(seed), 8)
    a_panels = scatter_about(streams_of[0], (N_ROW * P_SIZE * BLK, N_COL * K * BLK), 1.0, 6.0, ((0, 4), (1, 8)), jnp.float32)
    b_panels = scatter_about(streams_of[1], (N_COL * K * BLK, N_COL * Q * BLK), (TICKS * K * BLK) ** -0.5, 0.1875, ((0, 4), (1, 8)), jnp.float32)
    a_occupancy = touch_ends((jax.random.randint(streams_of[2], (N_ROW * P_SIZE, N_COL * K), 0, 3) < 2).astype(jnp.int32), jax.random.fold_in(streams_of[2], 1), 0, 1)
    b_occupancy = touch_ends((jax.random.randint(streams_of[3], (N_COL * K, N_COL * Q), 0, 3) < 2).astype(jnp.int32), jax.random.fold_in(streams_of[3], 1), 0, 1)
    owner_device_keys = jax.random.split(jax.random.fold_in(streams_of[4], 1), N_ROW * N_COL * NBLK // NBLK)
    owner_device_turns = jax.random.permutation(jax.random.fold_in(streams_of[4], 3), N_ROW * N_COL * NBLK // NBLK)
    owner_device = jax.vmap(lambda own, number: shared_out(jax.random.fold_in(streams_of[4], 2), own, number, NBLK, N_ROW * N_COL, 1, CAP, 2))(owner_device_keys, owner_device_turns).reshape((N_ROW, N_COL, NBLK, 1))
    owner_block = touch_ends(jax.random.randint(streams_of[5], (N_ROW, N_COL, NBLK), 0, OWN), jax.random.fold_in(streams_of[5], 1), 0, OWN - 1).astype(jnp.int32)
    c_previous = scatter_about(streams_of[6], (N_ROW, N_COL, OWN, BLK, BLK), 1.0, 6.0, ((0, 4), (1, 8)), jnp.float32)
    return dict(a_panels=a_panels, b_panels=b_panels, a_occupancy=a_occupancy, b_occupancy=b_occupancy, owner_device=owner_device, owner_block=owner_block, c_previous=c_previous)


def reference(a_panels, b_panels, a_occupancy, b_occupancy, owner_device, owner_block, c_previous):
    a_mask = jnp.repeat(jnp.repeat(a_occupancy.astype(jnp.float32), BLK, axis=0), BLK, axis=1)
    b_mask = jnp.repeat(jnp.repeat(b_occupancy.astype(jnp.float32), BLK, axis=0), BLK, axis=1)
    a_eff = a_panels * a_mask
    b_eff = b_panels * b_mask
    a_four = a_eff.reshape(N_ROW, P_SIZE * BLK, N_COL, K * BLK).transpose(0, 2, 1, 3)
    b_four = b_eff.reshape(N_COL, K * BLK, N_COL, Q * BLK).transpose(0, 2, 1, 3)
    start = c_previous.reshape(N_ROW * N_COL * OWN, BLK, BLK)

    def one_device(total, index):
        row_i = index // N_COL
        col_j = index % N_COL
        acc = jnp.zeros((P_SIZE * BLK, Q * BLK), jnp.float32)
        for tick in range(TICKS):
            left = a_four[row_i, (col_j + tick) % N_COL]
            slot = ((row_i + col_j + tick) % N_COL) // N_ROW
            stored = (((row_i + tick) % N_ROW) * IMAGES + slot).astype(jnp.int32)
            right = b_four[stored, col_j]
            acc = acc + jnp.dot(left, right, preferred_element_type=jnp.float32, precision=lax.Precision.HIGHEST)
        pieces = acc.reshape(P_SIZE, BLK, Q, BLK).transpose(0, 2, 1, 3).reshape(NBLK, BLK, BLK)
        owners = owner_device[row_i, col_j, :, 0].astype(jnp.int32)
        targets = owner_block[row_i, col_j].astype(jnp.int32)
        places = (owners * OWN + targets).astype(jnp.int32)
        return total.at[places].add(pieces), None

    total, unused = lax.scan(one_device, start, jnp.arange(N_ROW * N_COL, dtype=jnp.int32))
    return total.reshape(N_ROW, N_COL, OWN, BLK, BLK)
```

```python
import functools

import jax
import jax.numpy as jnp
import numpy as np
from jax import lax
from jax.experimental import pallas as pl
from jax.experimental.pallas import tpu as pltpu
from jax.sharding import PartitionSpec as P

BLK = 128
TICKS = 4
VMEM_LIMIT = 48 * 1024 * 1024


def widen(occupancy, panel):
    return panel * jnp.repeat(jnp.repeat(occupancy.astype(jnp.float32), BLK, axis=0), BLK, axis=1)


def after(value, *others):
    return lax.optimization_barrier((value,) + others)[0]


def up_step(value, sources, step, n_row):
    pairs = [(b + step - 1, b + step) for b in sources if b + step < n_row]
    return lax.ppermute(value, "row", pairs) if pairs else None


def down_step(value, sources, step):
    pairs = [(b - step + 1, b - step) for b in sources if b - step >= 0]
    return lax.ppermute(value, "row", pairs) if pairs else None


def visit_order(n_row):
    return [sorted(range(n_row), key=lambda i: (abs(i - r), i < r)) for r in range(n_row)]


def image_key(row, inner, n_row):
    source, kind = inner % n_row, "XY"[inner // n_row]
    return (kind, source - row)


def split(value):
    high = value.astype(jnp.bfloat16)
    low = (value - high.astype(jnp.float32)).astype(jnp.bfloat16)
    return high, low


def product_kernel(place, choices, table, which, *refs):
    count = len(choices)
    lefts = refs[:TICKS]
    rights = refs[TICKS : TICKS + count]
    out = refs[TICKS + count]
    left_in, right_in, left_hi, left_lo, right_hi, right_lo, left_sem, right_sem = refs[TICKS + count + 1 :]
    inner = right_in.shape[1]
    q_blocks = right_in.shape[2] // BLK

    def left_copy(t):
        return pltpu.make_async_copy(lefts[t].at[place], left_in.at[t], left_sem.at[t])

    for t in range(TICKS):
        left_copy(t).start()
        for position, (ref, ticks) in enumerate(zip(rights, choices)):
            if t in ticks:

                @pl.when(which[t] == position)
                def _():
                    pltpu.make_async_copy(ref, right_in.at[t], right_sem.at[t]).start()

    for t in range(TICKS):
        left_copy(t).wait()
        pltpu.make_async_copy(rights[0], right_in.at[t], right_sem.at[t]).wait()
        cols = pl.ds(t * inner, inner)

        @pl.loop(0, left_in.shape[1] // BLK)
        def _(p):
            rows = pl.ds(pl.multiple_of(p * BLK, BLK), BLK)
            left_hi[rows, cols], left_lo[rows, cols] = split(left_in[t, rows, :])

        @pl.loop(0, inner // 32)
        def _(p):
            rows = pl.ds(pl.multiple_of(p * 32, 32), 32)
            to = pl.ds(pl.multiple_of(t * inner + p * 32, 32), 32)
            right_hi[to, :], right_lo[to, :] = split(right_in[t, rows, :])

    @pl.loop(0, out.shape[0])
    def _(slot):
        block = table[slot]

        @pl.when(block >= 0)
        def _():
            rows = pl.ds(pl.multiple_of((block // q_blocks) * BLK, BLK), BLK)
            cols = pl.ds(pl.multiple_of((block % q_blocks) * BLK, BLK), BLK)
            dot = functools.partial(jnp.dot, preferred_element_type=jnp.float32)
            high, low = left_hi[rows, :], right_lo[:, cols]
            small = dot(high, low)
            other = right_hi[:, cols]
            small = small + dot(left_lo[rows, :], other)
            out[slot] = small + dot(high, other)

        @pl.when(block < 0)
        def _():
            out[slot] = jnp.zeros((BLK, BLK), jnp.float32)


def products(table, which, lefts, rights, choices, place, slots):
    rows, inner = lefts[0].shape[1:]
    cols = rights[0].shape[1]
    smem = pl.BlockSpec(memory_space=pltpu.SMEM)
    hbm = pl.BlockSpec(memory_space=pl.ANY)
    deep = TICKS * inner
    return pl.pallas_call(
        functools.partial(product_kernel, place, choices),
        out_shape=jax.ShapeDtypeStruct((slots, BLK, BLK), jnp.float32),
        in_specs=[smem, smem] + [hbm] * (TICKS + len(rights)),
        out_specs=pl.BlockSpec(memory_space=pltpu.VMEM),
        scratch_shapes=[
            pltpu.VMEM((TICKS, rows, inner), jnp.float32),
            pltpu.VMEM((TICKS, inner, cols), jnp.float32),
            pltpu.VMEM((rows, deep), jnp.bfloat16),
            pltpu.VMEM((rows, deep), jnp.bfloat16),
            pltpu.VMEM((deep, cols), jnp.bfloat16),
            pltpu.VMEM((deep, cols), jnp.bfloat16),
            pltpu.SemaphoreType.DMA((TICKS,)),
            pltpu.SemaphoreType.DMA((TICKS,)),
        ],
        compiler_params=pltpu.CompilerParams(vmem_limit_bytes=VMEM_LIMIT),
        cost_estimate=pl.CostEstimate(
            flops=2 * 6 * slots * BLK * BLK * deep,
            bytes_accessed=4 * (deep * (rows + cols) + slots * BLK * BLK),
            transcendentals=0,
        ),
        name="products",
    )(table, which, *lefts, *rights)


def add_kernel(targets, got, start, out):
    out[...] = start[...]

    @pl.loop(0, got.shape[0])
    def _(slot):
        target = targets[slot]

        @pl.when(target >= 0)
        def _():
            out[target] = out[target] + got[slot]


def add_blocks(targets, got, start):
    vmem = pl.BlockSpec(memory_space=pltpu.VMEM)
    return pl.pallas_call(
        add_kernel,
        out_shape=jax.ShapeDtypeStruct(start.shape, jnp.float32),
        in_specs=[pl.BlockSpec(memory_space=pltpu.SMEM), vmem, vmem],
        out_specs=vmem,
        compiler_params=pltpu.CompilerParams(vmem_limit_bytes=VMEM_LIMIT),
        cost_estimate=pl.CostEstimate(
            flops=got.size, bytes_accessed=4 * (got.size + 2 * start.size), transcendentals=0
        ),
        name="add_blocks",
    )(targets, got, start)


def tables(owner_device, owner_block, n_row, n_col, capacity):
    row, col = lax.axis_index("row"), lax.axis_index("col")
    mine = jnp.stack([owner_device.reshape(-1), owner_block.reshape(-1)])
    every = lax.all_gather(mine, ("row", "col"))
    count = mine.shape[1]
    every = every.reshape(n_row, n_col, 2, count)
    places = jnp.arange(capacity, dtype=jnp.int32)

    def spread(match, values):
        rank = jnp.cumsum(match.astype(jnp.int32), axis=-1) - 1
        hit = match[..., None, :] & (rank[..., None, :] == places[:, None])
        return jnp.max(jnp.where(hit, values[..., None, :], -1), axis=-1)

    column = lax.dynamic_index_in_dim(every[:, :, 0], col, axis=1, keepdims=False)
    owners = row * n_col + jnp.arange(n_col, dtype=jnp.int32)
    numbers = jnp.arange(count, dtype=jnp.int32)
    sent = spread(
        column[:, None, :] == owners[None, :, None],
        jnp.broadcast_to(numbers, (n_row, n_col, count)),
    )
    got = spread(every[:, :, 0] == row * n_col + col, every[:, :, 1])
    return sent.reshape(n_row, n_col * capacity), got.reshape(n_row, n_col * capacity)


def per_device(a_panels, b_panels, a_occupancy, b_occupancy, owner_device, owner_block, c_previous):
    n_row = lax.axis_size("row")
    n_col = lax.axis_size("col")
    row, col = lax.axis_index("row"), lax.axis_index("col")
    images = n_col // n_row
    inner = b_panels.shape[0] // images
    count_blocks = owner_block.size
    capacity = max(2, (2 * count_blocks + n_row * n_col - 1) // (n_row * n_col))
    order = visit_order(n_row)

    left = widen(a_occupancy, a_panels)
    right = widen(b_occupancy, b_panels)

    def image(number):
        slot = (row + col + number * n_row) % n_col // n_row
        return lax.dynamic_slice_in_dim(right, slot * inner, inner, 0)

    held = {("X", 0): image(0), ("Y", 0): image(1)}
    panels = {0: left}
    every_row = list(range(n_row))
    early = list(range(TICKS - 1))

    sent, got = tables(owner_device, owner_block, n_row, n_col, capacity)
    for d in range(1, n_row):
        panels[-d] = up_step(panels[1 - d], every_row, d, n_row)
        panels[d] = down_step(panels[d - 1], every_row, d)
        held["Y", -d] = up_step(held["Y", 1 - d], early, d, n_row)
        held["X", d] = down_step(held["X", d - 1], every_row, d)
    gate = (held["Y", 2 - n_row], held["X", n_row - 2])
    later = {("X", 0): after(held["X", 0], *gate), ("Y", 0): after(held["Y", 0], *gate)}
    for d in range(1, n_row):
        held["X", -d] = later["X", -d] = up_step(later["X", 1 - d], every_row, d, n_row)
        if d < TICKS - 1:
            held["Y", d] = later["Y", d] = down_step(later["Y", d - 1], early, d)

    backward = [((c + 1) % n_col, c) for c in range(n_col)]

    def chosen(step):
        offsets = [order[r][step] - r for r in range(n_row)]
        kinds = sorted(set(offsets))
        index = jnp.asarray([kinds.index(o) for o in offsets], jnp.int32)[row]
        return lax.select_n(index, *[panels[k] for k in kinds]) if len(kinds) > 2 else lax.select_n(
            index == len(kinds) - 1, *[panels[k] for k in kinds]
        )

    first = [left[None]]
    rest = [jnp.stack([chosen(step) for step in range(1, n_row)])]
    for t in range(1, TICKS):
        first.append(lax.ppermute(first[-1], "col", backward))
    for t in range(1, TICKS):
        rest.append(lax.ppermute(rest[-1], "col", backward))

    total = c_previous.reshape(c_previous.shape[2:])
    for step in range(n_row):
        keys = [[image_key(r, order[r][step] + t, n_row) for t in range(TICKS)] for r in range(n_row)]
        names = sorted({key for of_row in keys for key in of_row})
        choices = [{t for r in range(n_row) for t in range(TICKS) if keys[r][t] == name} for name in names]
        which = jnp.asarray([[names.index(key) for key in of_row] for of_row in keys], jnp.int32)[row]
        visit = jnp.asarray([order[r][step] for r in range(n_row)], jnp.int32)[row]
        blocks = products(
            sent[visit],
            which,
            first if step == 0 else rest,
            [held[name] for name in names],
            choices,
            0 if step == 0 else step - 1,
            n_col * capacity,
        )
        arrived = lax.all_to_all(blocks, "col", split_axis=0, concat_axis=0, tiled=True)
        total = add_blocks(got[visit], arrived, total)
    return total.reshape(c_previous.shape)


def solution(mesh):
    in_specs = (
        P("row", "col"),
        P("row", "col"),
        P("row", "col"),
        P("row", "col"),
        P("row", "col", None, None),
        P("row", "col", None),
        P("row", "col", None, None, None),
    )
    out_specs = P("row", "col", None, None, None)
    return jax.shard_map(
        per_device, mesh=mesh, in_specs=in_specs, out_specs=out_specs, check_vma=False
    )
```

```python
import functools

import jax
import jax.numpy as jnp
import numpy as np
from jax import lax
from jax.experimental import pallas as pl
from jax.experimental.pallas import tpu as pltpu
from jax.sharding import PartitionSpec as P

BLK = 128
TICKS = 4
VMEM_LIMIT = 48 * 1024 * 1024


def widen(occupancy, panel):
    return panel * jnp.repeat(jnp.repeat(occupancy.astype(jnp.float32), BLK, axis=0), BLK, axis=1)


def up_step(value, sources, step, n_row):
    pairs = [(b + step - 1, b + step) for b in sources if b + step < n_row]
    return lax.ppermute(value, "row", pairs) if pairs else None


def down_step(value, sources, step):
    pairs = [(b - step + 1, b - step) for b in sources if b - step >= 0]
    return lax.ppermute(value, "row", pairs) if pairs else None


def visit_order(n_row):
    return [sorted(range(n_row), key=lambda i: (abs(i - r), i < r)) for r in range(n_row)]


def image_key(row, inner, n_row):
    source, kind = inner % n_row, "XY"[inner // n_row]
    return (kind, source - row)


def split(value):
    high = value.astype(jnp.bfloat16)
    low = (value - high.astype(jnp.float32)).astype(jnp.bfloat16)
    return high, low


def product_kernel(choices, table, which, *refs):
    count = len(choices)
    lefts = refs[:TICKS]
    rights = refs[TICKS : TICKS + count]
    out = refs[TICKS + count]
    left_in, right_in, left_hi, left_lo, right_hi, right_lo, left_sem, right_sem = refs[TICKS + count + 1 :]
    inner = right_in.shape[1]
    q_blocks = right_in.shape[2] // BLK

    def left_copy(t):
        return pltpu.make_async_copy(lefts[t], left_in.at[t], left_sem.at[t])

    for t in range(TICKS):
        left_copy(t).start()
        for position, (ref, ticks) in enumerate(zip(rights, choices)):
            if t in ticks:

                @pl.when(which[t] == position)
                def _():
                    pltpu.make_async_copy(ref, right_in.at[t], right_sem.at[t]).start()

    for t in range(TICKS):
        left_copy(t).wait()
        pltpu.make_async_copy(rights[0], right_in.at[t], right_sem.at[t]).wait()
        cols = pl.ds(t * inner, inner)

        @pl.loop(0, left_in.shape[1] // BLK)
        def _(p):
            rows = pl.ds(pl.multiple_of(p * BLK, BLK), BLK)
            left_hi[rows, cols], left_lo[rows, cols] = split(left_in[t, rows, :])

        @pl.loop(0, inner // 32)
        def _(p):
            rows = pl.ds(pl.multiple_of(p * 32, 32), 32)
            to = pl.ds(pl.multiple_of(t * inner + p * 32, 32), 32)
            right_hi[to, :], right_lo[to, :] = split(right_in[t, rows, :])

    @pl.loop(0, out.shape[0])
    def _(slot):
        block = table[slot]

        @pl.when(block >= 0)
        def _():
            rows = pl.ds(pl.multiple_of((block // q_blocks) * BLK, BLK), BLK)
            cols = pl.ds(pl.multiple_of((block % q_blocks) * BLK, BLK), BLK)
            dot = functools.partial(jnp.dot, preferred_element_type=jnp.float32)
            high, low = left_hi[rows, :], right_lo[:, cols]
            small = dot(high, low)
            other = right_hi[:, cols]
            small = small + dot(left_lo[rows, :], other)
            out[slot] = small + dot(high, other)

        @pl.when(block < 0)
        def _():
            out[slot] = jnp.zeros((BLK, BLK), jnp.float32)


def products(table, which, lefts, rights, choices, slots):
    rows, inner = lefts[0].shape
    cols = rights[0].shape[1]
    smem = pl.BlockSpec(memory_space=pltpu.SMEM)
    hbm = pl.BlockSpec(memory_space=pl.ANY)
    deep = TICKS * inner
    return pl.pallas_call(
        functools.partial(product_kernel, choices),
        out_shape=jax.ShapeDtypeStruct((slots, BLK, BLK), jnp.float32),
        in_specs=[smem, smem] + [hbm] * (TICKS + len(rights)),
        out_specs=pl.BlockSpec(memory_space=pltpu.VMEM),
        scratch_shapes=[
            pltpu.VMEM((TICKS, rows, inner), jnp.float32),
            pltpu.VMEM((TICKS, inner, cols), jnp.float32),
            pltpu.VMEM((rows, deep), jnp.bfloat16),
            pltpu.VMEM((rows, deep), jnp.bfloat16),
            pltpu.VMEM((deep, cols), jnp.bfloat16),
            pltpu.VMEM((deep, cols), jnp.bfloat16),
            pltpu.SemaphoreType.DMA((TICKS,)),
            pltpu.SemaphoreType.DMA((TICKS,)),
        ],
        compiler_params=pltpu.CompilerParams(vmem_limit_bytes=VMEM_LIMIT),
        cost_estimate=pl.CostEstimate(
            flops=2 * 6 * slots * BLK * BLK * deep,
            bytes_accessed=4 * (deep * (rows + cols) + slots * BLK * BLK),
            transcendentals=0,
        ),
        name="products",
    )(table, which, *lefts, *rights)


def add_kernel(targets, got, start, out):
    out[...] = start[...]

    @pl.loop(0, got.shape[0])
    def _(slot):
        target = targets[slot]

        @pl.when(target >= 0)
        def _():
            out[target] = out[target] + got[slot]


def add_blocks(targets, got, start):
    vmem = pl.BlockSpec(memory_space=pltpu.VMEM)
    return pl.pallas_call(
        add_kernel,
        out_shape=jax.ShapeDtypeStruct(start.shape, jnp.float32),
        in_specs=[pl.BlockSpec(memory_space=pltpu.SMEM), vmem, vmem],
        out_specs=vmem,
        compiler_params=pltpu.CompilerParams(vmem_limit_bytes=VMEM_LIMIT),
        cost_estimate=pl.CostEstimate(
            flops=got.size, bytes_accessed=4 * (got.size + 2 * start.size), transcendentals=0
        ),
        name="add_blocks",
    )(targets, got, start)


def tables(owner_device, owner_block, n_row, n_col, capacity):
    row, col = lax.axis_index("row"), lax.axis_index("col")
    mine = jnp.stack([owner_device.reshape(-1), owner_block.reshape(-1)])
    count = mine.shape[1]
    every = lax.all_to_all(
        jnp.broadcast_to(mine, (n_row * n_col,) + mine.shape), ("row", "col"), 0, 0, tiled=True
    )
    every = every.reshape(n_row, n_col, 2, count)
    places = jnp.arange(capacity, dtype=jnp.int32)

    def spread(match, values):
        rank = jnp.cumsum(match.astype(jnp.int32), axis=-1) - 1
        hit = match[..., None, :] & (rank[..., None, :] == places[:, None])
        return jnp.max(jnp.where(hit, values[..., None, :], -1), axis=-1)

    column = lax.dynamic_index_in_dim(every[:, :, 0], col, axis=1, keepdims=False)
    owners = row * n_col + jnp.arange(n_col, dtype=jnp.int32)
    numbers = jnp.arange(count, dtype=jnp.int32)
    sent = spread(
        column[:, None, :] == owners[None, :, None],
        jnp.broadcast_to(numbers, (n_row, n_col, count)),
    )
    got = spread(every[:, :, 0] == row * n_col + col, every[:, :, 1])
    return sent.reshape(n_row, n_col * capacity), got.reshape(n_row, n_col * capacity)


def per_device(a_panels, b_panels, a_occupancy, b_occupancy, owner_device, owner_block, c_previous):
    n_row = lax.axis_size("row")
    n_col = lax.axis_size("col")
    row, col = lax.axis_index("row"), lax.axis_index("col")
    images = n_col // n_row
    inner = b_panels.shape[0] // images
    count_blocks = owner_block.size
    capacity = max(2, (2 * count_blocks + n_row * n_col - 1) // (n_row * n_col))
    order = visit_order(n_row)
    every_row = list(range(n_row))
    early = list(range(TICKS - 1))
    backward = [((c + 1) % n_col, c) for c in range(n_col)]

    def image(number):
        slot = (row + col + number * n_row) % n_col // n_row
        present = lax.dynamic_slice_in_dim(b_occupancy, slot * (inner // BLK), inner // BLK, 0)
        return widen(present, lax.dynamic_slice_in_dim(b_panels, slot * inner, inner, 0))

    held = {("A", 0): widen(a_occupancy, a_panels), ("X", 0): image(0), ("Y", 0): image(1)}

    def chosen(step):
        offsets = [order[r][step] - r for r in range(n_row)]
        kinds = sorted(set(offsets))
        index = jnp.asarray([kinds.index(o) for o in offsets], jnp.int32)[row]
        cases = [held["A", k] for k in kinds]
        return cases[0] if len(cases) == 1 else lax.select_n(
            index if len(cases) > 2 else index == 1, *cases
        )

    sent = got = None
    lefts = []
    total = c_previous.reshape(c_previous.shape[2:])
    for phase in range(1, 2 * n_row):
        moving = {}
        d = phase if phase < n_row else phase - n_row + 1
        if d < n_row:
            upward, downward = ("AY", "AX") if phase < n_row else ("X", "Y")
            for kind in upward:
                sources = early if kind == "Y" else every_row
                moving[kind, -d] = up_step(held[kind, 1 - d], sources, d, n_row)
            for kind in downward:
                sources = early if kind == "Y" else every_row
                if (kind, d - 1) in held:
                    moving[kind, d] = down_step(held[kind, d - 1], sources, d)
        if phase <= n_row:
            lefts.append([chosen(phase - 1)])
        for step, panels in enumerate(lefts):
            if len(panels) < TICKS:
                moving["left", step] = lax.ppermute(panels[-1], "col", backward)
        if phase == 1:
            sent, got = tables(owner_device, owner_block, n_row, n_col, capacity)
        step = phase - n_row
        if step >= 0:
            keys = [
                [image_key(r, order[r][step] + t, n_row) for t in range(TICKS)] for r in range(n_row)
            ]
            names = sorted({key for of_row in keys for key in of_row})
            choices = [
                {t for r in range(n_row) for t in range(TICKS) if keys[r][t] == name} for name in names
            ]
            index = [[names.index(key) for key in of_row] for of_row in keys]
            which = jnp.asarray(index, jnp.int32)[row]
            visit = jnp.asarray([order[r][step] for r in range(n_row)], jnp.int32)[row]
            blocks = products(
                sent[visit],
                which,
                lefts[step],
                [held[name] for name in names],
                choices,
                n_col * capacity,
            )
            arrived = lax.all_to_all(blocks, "col", split_axis=0, concat_axis=0, tiled=True)
            total = add_blocks(got[visit], arrived, total)
        moving = {key: value for key, value in moving.items() if value is not None}
        if moving:
            names = list(moving) + [key for key in held if key not in moving]
            values = [moving.get(key, held.get(key)) for key in names]
            values = lax.optimization_barrier(tuple(values) + (sent,))
            sent = values[-1]
            for key, value in zip(names, values):
                if key[0] == "left":
                    lefts[key[1]].append(value)
                else:
                    held[key] = value
    return total.reshape(c_previous.shape)


def solution(mesh):
    in_specs = (
        P("row", "col"),
        P("row", "col"),
        P("row", "col"),
        P("row", "col"),
        P("row", "col", None, None),
        P("row", "col", None),
        P("row", "col", None, None, None),
    )
    out_specs = P("row", "col", None, None, None)
    return jax.shard_map(
        per_device, mesh=mesh, in_specs=in_specs, out_specs=out_specs, check_vma=False
    )
```

```python
import functools

import jax
import jax.numpy as jnp
import numpy as np
from jax import lax
from jax.experimental import pallas as pl
from jax.experimental.pallas import tpu as pltpu
from jax.sharding import PartitionSpec as P

BLK = 128
TICKS = 4
PARTS = 2
ABREAST = 8
VMEM_LIMIT = 48 * 1024 * 1024


def widen(occupancy, panel):
    return panel * jnp.repeat(jnp.repeat(occupancy.astype(jnp.float32), BLK, axis=0), BLK, axis=1)


def up_step(value, sources, step, n_row):
    pairs = [(b + step - 1, b + step) for b in sources if b + step < n_row]
    return lax.ppermute(value, "row", pairs) if pairs else None


def down_step(value, sources, step):
    pairs = [(b - step + 1, b - step) for b in sources if b - step >= 0]
    return lax.ppermute(value, "row", pairs) if pairs else None


def visit_order(n_row):
    return [sorted(range(n_row), key=lambda i: (abs(i - r), i < r)) for r in range(n_row)]


def image_key(row, inner, n_row):
    source, kind = inner % n_row, "XY"[inner // n_row]
    return (kind, source - row)


def split(value):
    high = value.astype(jnp.bfloat16)
    low = (value - high.astype(jnp.float32)).astype(jnp.bfloat16)
    return high, low


def product_kernel(place, choices, table, full, used, which, *refs):
    count = len(choices) * PARTS
    lefts = refs[:TICKS]
    rights = refs[TICKS : TICKS + count]
    out = refs[TICKS + count]
    left_in, right_in, left_two, right_two, left_sem, right_sem = refs[TICKS + count + 1 :]
    inner = right_in.shape[1]
    q_blocks = right_in.shape[2] // BLK

    def left_copy(t):
        return pltpu.make_async_copy(lefts[t].at[place], left_in.at[t], left_sem.at[t])

    for t in range(TICKS):
        left_copy(t).start()
        for position, ticks in enumerate(choices):
            of_image = rights[position * PARTS : (position + 1) * PARTS]
            if t in ticks:

                @pl.when(which[t] == position)
                def _():
                    for part, ref in enumerate(of_image):
                        rows = pl.ds(part * ref.shape[0], ref.shape[0])
                        pltpu.make_async_copy(ref, right_in.at[t, rows], right_sem.at[t]).start()

    for t in range(TICKS):
        left_copy(t).wait()
        pltpu.make_async_copy(right_in.at[t], right_in.at[t], right_sem.at[t]).wait()
        cols = pl.ds(t * inner, inner)

        @pl.loop(0, left_in.shape[1] // BLK)
        def _(p):
            rows = pl.ds(pl.multiple_of(p * BLK, BLK), BLK)
            high, low = split(left_in[t, rows, :])
            left_two[pl.ds(pl.multiple_of(p * 2 * BLK, 2 * BLK), BLK), cols] = high
            left_two[pl.ds(pl.multiple_of(p * 2 * BLK + BLK, BLK), BLK), cols] = low

        @pl.loop(0, inner // 32)
        def _(p):
            rows = pl.ds(pl.multiple_of(p * 32, 32), 32)
            to = pl.ds(pl.multiple_of(t * inner + p * 32, 32), 32)
            for q in range(q_blocks):
                high, low = split(right_in[t, rows, q * BLK : (q + 1) * BLK])
                right_two[to, 2 * q * BLK : (2 * q + 1) * BLK] = high
                right_two[to, (2 * q + 1) * BLK : (2 * q + 2) * BLK] = low

    def one(slot):
        block = jnp.maximum(table[slot], 0)
        rows = pl.ds(pl.multiple_of((block // q_blocks) * 2 * BLK, 2 * BLK), 2 * BLK)
        cols = pl.ds(pl.multiple_of((block % q_blocks) * 2 * BLK, 2 * BLK), 2 * BLK)
        four = jnp.dot(left_two[rows, :], right_two[:, cols], preferred_element_type=jnp.float32)
        out[slot] = (four[:BLK, :BLK] + (four[:BLK, BLK:] + four[BLK:, :BLK])) + four[BLK:, BLK:]

    @pl.loop(0, (used[0] + ABREAST - 1) // ABREAST)
    def _(turn):
        for extra in range(ABREAST):
            one(full[turn * ABREAST + extra])


def products(slots_used, which, lefts, rights, choices, place, slots):
    rows, inner = lefts[0].shape[-2:]
    cols = rights[0][0].shape[1]
    rights = [part for of_image in rights for part in of_image]
    smem = pl.BlockSpec(memory_space=pltpu.SMEM)
    hbm = pl.BlockSpec(memory_space=pl.ANY)
    deep = TICKS * inner
    return pl.pallas_call(
        functools.partial(product_kernel, place, choices),
        out_shape=jax.ShapeDtypeStruct((slots, BLK, BLK), jnp.float32),
        in_specs=[smem] * 4 + [hbm] * (TICKS + len(rights)),
        out_specs=pl.BlockSpec(memory_space=pltpu.VMEM),
        scratch_shapes=[
            pltpu.VMEM((TICKS, rows, inner), jnp.float32),
            pltpu.VMEM((TICKS, inner, cols), jnp.float32),
            pltpu.VMEM((2 * rows, deep), jnp.bfloat16),
            pltpu.VMEM((deep, 2 * cols), jnp.bfloat16),
            pltpu.SemaphoreType.DMA((TICKS,)),
            pltpu.SemaphoreType.DMA((TICKS,)),
        ],
        compiler_params=pltpu.CompilerParams(vmem_limit_bytes=VMEM_LIMIT),
        cost_estimate=pl.CostEstimate(
            flops=2 * 6 * slots * BLK * BLK * deep,
            bytes_accessed=4 * (deep * (rows + cols) + slots * BLK * BLK),
            transcendentals=0,
        ),
        name="products",
    )(*slots_used, which, *lefts, *rights)


def add_kernel(targets, leader, got, start, out, got_in, total, got_sem, start_sem, out_sem):
    slots = got.shape[0]

    def got_copy(slot):
        return pltpu.make_async_copy(got.at[slot], got_in.at[slot], got_sem.at[slot])

    def start_copy(slot):
        return pltpu.make_async_copy(out.at[targets[slot]], total.at[slot], start_sem.at[slot])

    def out_copy(slot):
        return pltpu.make_async_copy(total.at[slot], out.at[targets[slot]], out_sem.at[slot])

    def every(leads, work):
        @pl.loop(0, slots)
        def _(slot):
            there = targets[slot] >= 0
            if leads:
                there = jnp.logical_and(there, leader[slot] == slot)

            @pl.when(there)
            def _():
                work(slot)

    every(True, lambda slot: start_copy(slot).start())
    every(False, lambda slot: got_copy(slot).start())
    every(True, lambda slot: start_copy(slot).wait())

    def add(slot):
        got_copy(slot).wait()
        total[leader[slot]] = total[leader[slot]] + got_in[slot]

    every(False, add)
    every(True, lambda slot: out_copy(slot).start())
    every(True, lambda slot: out_copy(slot).wait())


def add_blocks(targets, leader, got, start):
    smem = pl.BlockSpec(memory_space=pltpu.SMEM)
    hbm = pl.BlockSpec(memory_space=pl.ANY)
    slots = got.shape[0]
    return pl.pallas_call(
        add_kernel,
        out_shape=jax.ShapeDtypeStruct(start.shape, jnp.float32),
        in_specs=[smem, smem, hbm, hbm],
        out_specs=hbm,
        input_output_aliases={3: 0},
        scratch_shapes=[
            pltpu.VMEM(got.shape, jnp.float32),
            pltpu.VMEM(got.shape, jnp.float32),
            pltpu.SemaphoreType.DMA((slots,)),
            pltpu.SemaphoreType.DMA((slots,)),
            pltpu.SemaphoreType.DMA((slots,)),
        ],
        compiler_params=pltpu.CompilerParams(vmem_limit_bytes=VMEM_LIMIT),
        cost_estimate=pl.CostEstimate(
            flops=got.size, bytes_accessed=4 * 3 * got.size, transcendentals=0
        ),
        name="add_blocks",
    )(targets, leader, got, start)


def first_kernel(targets, got, start, out):
    out[...] = start[...]

    @pl.loop(0, got.shape[0])
    def _(slot):
        target = targets[slot]

        @pl.when(target >= 0)
        def _():
            out[target] = out[target] + got[slot]


def first_blocks(targets, got, start):
    vmem = pl.BlockSpec(memory_space=pltpu.VMEM)
    return pl.pallas_call(
        first_kernel,
        out_shape=jax.ShapeDtypeStruct(start.shape, jnp.float32),
        in_specs=[pl.BlockSpec(memory_space=pltpu.SMEM), vmem, vmem],
        out_specs=vmem,
        compiler_params=pltpu.CompilerParams(vmem_limit_bytes=VMEM_LIMIT),
        cost_estimate=pl.CostEstimate(
            flops=got.size, bytes_accessed=4 * (got.size + 2 * start.size), transcendentals=0
        ),
        name="first_blocks",
    )(targets, got, start)


def tables(every, n_row, n_col, capacity):
    row, col = lax.axis_index("row"), lax.axis_index("col")
    count = every.shape[-1]
    every = every.reshape(n_row, n_col, 2, count)
    places = jnp.arange(capacity, dtype=jnp.int32)

    def spread(match, values):
        rank = jnp.cumsum(match.astype(jnp.int32), axis=-1) - 1
        hit = match[..., None, :] & (rank[..., None, :] == places[:, None])
        return jnp.max(jnp.where(hit, values[..., None, :], -1), axis=-1)

    column = lax.dynamic_index_in_dim(every[:, :, 0], col, axis=1, keepdims=False)
    owners = row * n_col + jnp.arange(n_col, dtype=jnp.int32)
    numbers = jnp.arange(count, dtype=jnp.int32)
    sent = spread(
        column[:, None, :] == owners[None, :, None],
        jnp.broadcast_to(numbers, (n_row, n_col, count)),
    )
    got = spread(every[:, :, 0] == row * n_col + col, every[:, :, 1])
    sent, got = (value.reshape(n_row, n_col * capacity) for value in (sent, got))
    slots = jnp.arange(n_col * capacity, dtype=jnp.int32)

    used = jnp.sum((sent >= 0).astype(jnp.int32), axis=-1, keepdims=True)
    rank = jnp.cumsum((sent >= 0).astype(jnp.int32), axis=-1)
    wanted = jnp.minimum(slots + 1, used)
    full = jnp.argmax(rank[:, None, :] >= wanted[..., None], axis=-1).astype(jnp.int32)
    leader = jnp.argmax(got[:, :, None] == got[:, None, :], axis=-1).astype(jnp.int32)
    return {"sent": sent, "full": full, "used": used, "got": got, "leader": leader}


def per_device(a_panels, b_panels, a_occupancy, b_occupancy, owner_device, owner_block, c_previous):
    n_row = lax.axis_size("row")
    n_col = lax.axis_size("col")
    row, col = lax.axis_index("row"), lax.axis_index("col")
    images = n_col // n_row
    inner = b_panels.shape[0] // images
    count_blocks = owner_block.size
    capacity = max(2, (2 * count_blocks + n_row * n_col - 1) // (n_row * n_col))
    order = visit_order(n_row)
    every_row = list(range(n_row))
    early = list(range(TICKS - 1))
    backward = [((c + 1) % n_col, c) for c in range(n_col)]

    def image(number, part):
        depth = inner // PARTS
        start = (row + col + number * n_row) % n_col // n_row * inner + part * depth
        present = lax.dynamic_slice_in_dim(b_occupancy, start // BLK, depth // BLK, 0)
        return widen(present, lax.dynamic_slice_in_dim(b_panels, start, depth, 0))

    held = {("A", 0, 0): widen(a_occupancy, a_panels)}
    for part in range(PARTS):
        held["Y", part, 0] = image(1, part)
        held["X", part, 0] = image(0, part)
    mine = jnp.stack([owner_device.reshape(-1), owner_block.reshape(-1)])
    held["owners"] = jnp.broadcast_to(mine, (n_row * n_col,) + mine.shape)

    first = [(("A", 0, -d), ("A", 0, d)) for d in range(1, n_row)]
    lower = [(("Y", part, -d), ("X", part, d)) for d in range(1, n_row) for part in range(PARTS)]
    steps = []
    for number in range(max(len(first), len(lower))):
        steps += first[number : number + 1] + lower[number : number + 1]
    steps += [(("X", part, -d), ("Y", part, d)) for d in range(1, n_row) for part in range(PARTS)]
    ends = {keys[0]: number for number, keys in enumerate(steps)}

    def relay(key):
        kind, part, offset = key
        sources = early if kind == "Y" else every_row
        if offset < 0:
            return up_step(held[kind, part, offset + 1], sources, -offset, n_row)
        if (kind, part, offset - 1) in held:
            return down_step(held[kind, part, offset - 1], sources, offset)

    def close(due):
        held.update(due)
        held.update(zip(list(held), lax.optimization_barrier(tuple(held.values()))))

    def chosen(step):
        offsets = [order[r][step] - r for r in range(n_row)]
        kinds = sorted(set(offsets))
        index = jnp.asarray([kinds.index(o) for o in offsets], jnp.int32)[row]
        cases = [held["A", 0, k] for k in kinds]
        return lax.select_n(index if len(cases) > 2 else index == 1, *cases)

    def product(step):
        keys = [
            [image_key(r, order[r][step] + t, n_row) for t in range(TICKS)] for r in range(n_row)
        ]
        names = sorted({key for of_row in keys for key in of_row})
        choices = [
            {t for r in range(n_row) for t in range(TICKS) if keys[r][t] == name} for name in names
        ]
        index = [[names.index(key) for key in of_row] for of_row in keys]
        which = jnp.asarray(index, jnp.int32)[row]
        visit = jnp.asarray([order[r][step] for r in range(n_row)], jnp.int32)[row]
        return products(
            [held[name][visit] for name in ("sent", "full", "used")],
            which,
            [held["own" if step == 0 else "rest", t] for t in range(TICKS)],
            [[held[kind, part, offset] for part in range(PARTS)] for kind, offset in names],
            choices,
            max(step - 1, 0),
            n_col * capacity,
        )

    def exchange(step, total):
        visit = jnp.asarray([order[r][step] for r in range(n_row)], jnp.int32)[row]
        blocks = held["blocks", step]
        arrived = lax.all_to_all(blocks, "col", split_axis=0, concat_axis=0, tiled=True)
        targets, leader = held["got"][visit], held["leader"][visit]
        if step == 0:
            return first_blocks(targets, arrived, total)
        return add_blocks(targets, leader, arrived, total)

    held["own", 0] = held["A", 0, 0][None]
    start_of = {ends["Y", PARTS - 1, -(n_row - 1)] + 2: 0}
    for d in range(1, n_row):
        start_of[ends["X", PARTS - 1, -d] + 2] = d
    total = c_previous.reshape(c_previous.shape[2:])
    flying = {2: {}, 3: {}, 4: {}}
    for number in range(len(steps) + 2):
        if number >= 2:
            close(flying.pop(number))
        if number == 2:
            every = lax.all_to_all(held["owners"], ("row", "col"), 0, 0, tiled=True)
            flying[number + 2]["every"] = every
        if number == 4:
            flying[number + 1].update(tables(held["every"], n_row, n_col, capacity))
        if number - 1 in start_of:
            total = exchange(start_of[number - 1], total)
        if number < len(steps):
            moving = {key: relay(key) for key in steps[number]}
            flying.setdefault(number + 2, {}).update(
                {key: value for key, value in moving.items() if value is not None}
            )
        for name in ("own", "rest"):
            if name == "rest" and number == ends["A", 0, 1 - n_row] + 2:
                held["rest", 0] = jnp.stack([chosen(step) for step in range(1, n_row)])
            ahead = [t for t in range(1, TICKS) if (name, t) not in held]
            if ahead and (name, ahead[0] - 1) in held and not any(
                (name, ahead[0]) in of_step for of_step in flying.values()
            ):
                hop = lax.ppermute(held[name, ahead[0] - 1], "col", backward)
                flying.setdefault(number + 2, {})[name, ahead[0]] = hop
        if number in start_of:
            flying.setdefault(number + 1, {})["blocks", start_of[number]] = product(start_of[number])
    for due in flying.values():
        held.update(due)
    total = exchange(n_row - 1, total)
    return total.reshape(c_previous.shape)


def solution(mesh):
    in_specs = (
        P("row", "col"),
        P("row", "col"),
        P("row", "col"),
        P("row", "col"),
        P("row", "col", None, None),
        P("row", "col", None),
        P("row", "col", None, None, None),
    )
    out_specs = P("row", "col", None, None, None)
    return jax.shard_map(
        per_device, mesh=mesh, in_specs=in_specs, out_specs=out_specs, check_vma=False
    )
```

```python
import functools

import jax
import jax.numpy as jnp
import numpy as np
from jax import lax
from jax.experimental import pallas as pl
from jax.experimental.pallas import tpu as pltpu
from jax.sharding import PartitionSpec as P

BLK = 128
TICKS = 4
PARTS = 2
ABREAST = 8
VMEM_LIMIT = 48 * 1024 * 1024


def widen(occupancy, panel):
    return panel * jnp.repeat(jnp.repeat(occupancy.astype(jnp.float32), BLK, axis=0), BLK, axis=1)


def up_step(value, sources, step, n_row):
    pairs = [(b + step - 1, b + step) for b in sources if b + step < n_row]
    return lax.ppermute(value, "row", pairs) if pairs else None


def down_step(value, sources, step):
    pairs = [(b - step + 1, b - step) for b in sources if b - step >= 0]
    return lax.ppermute(value, "row", pairs) if pairs else None


def visit_order(n_row):
    return [sorted(range(n_row), key=lambda i: (abs(i - r), i < r)) for r in range(n_row)]


def image_key(row, inner, n_row):
    source, kind = inner % n_row, "XY"[inner // n_row]
    last = n_row - 1
    if kind == "X" and source < row:
        return ("C", source - row + (row < last))
    if kind == "Y" and source - row == -last:
        return ("C", 0)
    return (kind, source - row)


def split(value):
    high = value.astype(jnp.bfloat16)
    low = (value - high.astype(jnp.float32)).astype(jnp.bfloat16)
    return high, low


def product_kernel(place, choices, pieces, table, full, used, which, *refs):
    count = len(choices) * PARTS
    lefts = refs[:TICKS]
    rights = refs[TICKS : TICKS + count]
    outs = refs[TICKS + count : TICKS + count + pieces]
    left_in, right_in, left_two, right_two, out, left_sem, right_sem, out_sem = refs[TICKS + count + pieces :]
    inner = right_in.shape[1]
    q_blocks = right_in.shape[2] // BLK

    def left_copy(t):
        return pltpu.make_async_copy(lefts[t].at[place], left_in.at[t], left_sem.at[t])

    for t in range(TICKS):
        left_copy(t).start()
        for position, ticks in enumerate(choices):
            of_image = rights[position * PARTS : (position + 1) * PARTS]
            if t in ticks:

                @pl.when(which[t] == position)
                def _():
                    for part, ref in enumerate(of_image):
                        rows = pl.ds(part * ref.shape[0], ref.shape[0])
                        pltpu.make_async_copy(ref, right_in.at[t, rows], right_sem.at[t]).start()

    for t in range(TICKS):
        left_copy(t).wait()
        pltpu.make_async_copy(right_in.at[t], right_in.at[t], right_sem.at[t]).wait()
        cols = pl.ds(t * inner, inner)

        @pl.loop(0, left_in.shape[1] // BLK)
        def _(p):
            rows = pl.ds(pl.multiple_of(p * BLK, BLK), BLK)
            high, low = split(left_in[t, rows, :])
            left_two[pl.ds(pl.multiple_of(p * 2 * BLK, 2 * BLK), BLK), cols] = high
            left_two[pl.ds(pl.multiple_of(p * 2 * BLK + BLK, BLK), BLK), cols] = low

        @pl.loop(0, inner // 32)
        def _(p):
            rows = pl.ds(pl.multiple_of(p * 32, 32), 32)
            to = pl.ds(pl.multiple_of(t * inner + p * 32, 32), 32)
            for q in range(q_blocks):
                high, low = split(right_in[t, rows, q * BLK : (q + 1) * BLK])
                right_two[to, 2 * q * BLK : (2 * q + 1) * BLK] = high
                right_two[to, (2 * q + 1) * BLK : (2 * q + 2) * BLK] = low

    def one(slot):
        block = jnp.maximum(table[slot], 0)
        rows = pl.ds(pl.multiple_of((block // q_blocks) * 2 * BLK, 2 * BLK), 2 * BLK)
        cols = pl.ds(pl.multiple_of((block % q_blocks) * 2 * BLK, 2 * BLK), 2 * BLK)
        four = jnp.dot(left_two[rows, :], right_two[:, cols], preferred_element_type=jnp.float32)
        out[slot] = (four[:BLK, :BLK] + (four[:BLK, BLK:] + four[BLK:, :BLK])) + four[BLK:, BLK:]

    @pl.loop(0, (used[0] + ABREAST - 1) // ABREAST)
    def _(turn):
        for extra in range(ABREAST):
            one(full[turn * ABREAST + extra])

    copies = []
    for piece, ref in enumerate(outs):
        slots = pl.ds(piece * ref.shape[0], ref.shape[0])
        copies.append(pltpu.make_async_copy(out.at[slots], ref, out_sem.at[piece]))
        copies[-1].start()
    for copy in copies:
        copy.wait()


def products(slots_used, which, lefts, rights, choices, place, pieces):
    rows, inner = lefts[0].shape[-2:]
    cols = rights[0][0].shape[1]
    rights = [part for of_image in rights for part in of_image]
    smem = pl.BlockSpec(memory_space=pltpu.SMEM)
    hbm = pl.BlockSpec(memory_space=pl.ANY)
    deep = TICKS * inner
    slots = slots_used[0].shape[0]
    return pl.pallas_call(
        functools.partial(product_kernel, place, choices, pieces),
        out_shape=[jax.ShapeDtypeStruct((slots // pieces, BLK, BLK), jnp.float32)] * pieces,
        in_specs=[smem] * 4 + [hbm] * (TICKS + len(rights)),
        out_specs=[hbm] * pieces,
        scratch_shapes=[
            pltpu.VMEM((TICKS, rows, inner), jnp.float32),
            pltpu.VMEM((TICKS, inner, cols), jnp.float32),
            pltpu.VMEM((2 * rows, deep), jnp.bfloat16),
            pltpu.VMEM((deep, 2 * cols), jnp.bfloat16),
            pltpu.VMEM((slots, BLK, BLK), jnp.float32),
            pltpu.SemaphoreType.DMA((TICKS,)),
            pltpu.SemaphoreType.DMA((TICKS,)),
            pltpu.SemaphoreType.DMA((pieces,)),
        ],
        compiler_params=pltpu.CompilerParams(vmem_limit_bytes=VMEM_LIMIT),
        cost_estimate=pl.CostEstimate(
            flops=2 * 6 * slots * BLK * BLK * deep,
            bytes_accessed=4 * (deep * (rows + cols) + slots * BLK * BLK),
            transcendentals=0,
        ),
        name="products",
    )(*slots_used, which, *lefts, *rights)


def add_kernel(targets, leader, got, start, out, got_in, total, got_sem, start_sem, out_sem):
    slots = got.shape[0]

    def got_copy(slot):
        return pltpu.make_async_copy(got.at[slot], got_in.at[slot], got_sem.at[slot])

    def start_copy(slot):
        return pltpu.make_async_copy(out.at[targets[slot]], total.at[slot], start_sem.at[slot])

    def out_copy(slot):
        return pltpu.make_async_copy(total.at[slot], out.at[targets[slot]], out_sem.at[slot])

    def every(leads, work):
        @pl.loop(0, slots)
        def _(slot):
            there = targets[slot] >= 0
            if leads:
                there = jnp.logical_and(there, leader[slot] == slot)

            @pl.when(there)
            def _():
                work(slot)

    every(True, lambda slot: start_copy(slot).start())
    every(False, lambda slot: got_copy(slot).start())
    every(True, lambda slot: start_copy(slot).wait())

    def add(slot):
        got_copy(slot).wait()
        total[leader[slot]] = total[leader[slot]] + got_in[slot]

    every(False, add)
    every(True, lambda slot: out_copy(slot).start())
    every(True, lambda slot: out_copy(slot).wait())


def add_blocks(targets, leader, got, start):
    smem = pl.BlockSpec(memory_space=pltpu.SMEM)
    hbm = pl.BlockSpec(memory_space=pl.ANY)
    slots = got.shape[0]
    return pl.pallas_call(
        add_kernel,
        out_shape=jax.ShapeDtypeStruct(start.shape, jnp.float32),
        in_specs=[smem, smem, hbm, hbm],
        out_specs=hbm,
        input_output_aliases={3: 0},
        scratch_shapes=[
            pltpu.VMEM(got.shape, jnp.float32),
            pltpu.VMEM(got.shape, jnp.float32),
            pltpu.SemaphoreType.DMA((slots,)),
            pltpu.SemaphoreType.DMA((slots,)),
            pltpu.SemaphoreType.DMA((slots,)),
        ],
        compiler_params=pltpu.CompilerParams(vmem_limit_bytes=VMEM_LIMIT),
        cost_estimate=pl.CostEstimate(
            flops=got.size, bytes_accessed=4 * 3 * got.size, transcendentals=0
        ),
        name="add_blocks",
    )(targets, leader, got, start)


def first_kernel(targets, got, start, out):
    out[...] = start[...]

    @pl.loop(0, got.shape[0])
    def _(slot):
        target = targets[slot]

        @pl.when(target >= 0)
        def _():
            out[target] = out[target] + got[slot]


def first_blocks(targets, got, start):
    vmem = pl.BlockSpec(memory_space=pltpu.VMEM)
    return pl.pallas_call(
        first_kernel,
        out_shape=jax.ShapeDtypeStruct(start.shape, jnp.float32),
        in_specs=[pl.BlockSpec(memory_space=pltpu.SMEM), vmem, vmem],
        out_specs=vmem,
        compiler_params=pltpu.CompilerParams(vmem_limit_bytes=VMEM_LIMIT),
        cost_estimate=pl.CostEstimate(
            flops=got.size, bytes_accessed=4 * (got.size + 2 * start.size), transcendentals=0
        ),
        name="first_blocks",
    )(targets, got, start)


def tables(every, n_row, n_col, capacity, order):
    row, col = lax.axis_index("row"), lax.axis_index("col")
    count = every.shape[-1]
    every = every.reshape(n_row, n_col, 2, count)
    places = jnp.arange(capacity, dtype=jnp.int32)
    columns = jnp.arange(n_col, dtype=jnp.int32)
    visits = jnp.asarray(order, jnp.int32)[row]

    def spread(match, values):
        rank = jnp.cumsum(match.astype(jnp.int32), axis=-1) - 1
        hit = match[..., None, :] & (rank[..., None, :] == places[:, None])
        return jnp.max(jnp.where(hit, values[..., None, :], -1), axis=-1)

    column = lax.dynamic_index_in_dim(every[:, :, 0], col, axis=1, keepdims=False)[visits]
    numbers = jnp.arange(count, dtype=jnp.int32)

    def slots_of(blocks, owners):
        match = blocks[:, None, :] == owners[..., None]
        return spread(match, jnp.broadcast_to(numbers, match.shape)).reshape(len(blocks), -1)

    def listed(sent):
        there = (sent >= 0).astype(jnp.int32)
        used = jnp.sum(there, axis=-1, keepdims=True)
        rank = jnp.cumsum(there, axis=-1)
        wanted = jnp.minimum(jnp.arange(sent.shape[-1], dtype=jnp.int32) + 1, used)
        full = jnp.argmax(rank[:, None, :] >= wanted[..., None], axis=-1).astype(jnp.int32)
        return sent, full, used

    sent = listed(slots_of(column[:-1], jnp.broadcast_to(row * n_col + columns, (n_row - 1, n_col))))
    beside = jnp.where(row == 1, 0, jnp.where(row == n_row - 2, n_row - 1, -1))
    inside = jnp.where((row == 0) | (row == n_row - 1), -1, row)
    rows = jnp.stack([inside, beside])
    owners = jnp.where(rows[:, None] >= 0, rows[:, None] * n_col + columns, -1)
    final = listed(slots_of(column[-1:], owners.reshape(1, -1)))

    arriving = every[visits]
    got = spread(arriving[:, :, 0] == row * n_col + col, arriving[:, :, 1])
    got = got.reshape(n_row, n_col * capacity)
    leader = jnp.argmax(got[:, :, None] == got[:, None, :], axis=-1).astype(jnp.int32)
    names = ("sent", "full", "used", "last sent", "last full", "last used", "got", "leader")
    return dict(zip(names, (*sent, *final, got, leader)))


def per_device(a_panels, b_panels, a_occupancy, b_occupancy, owner_device, owner_block, c_previous):
    n_row = lax.axis_size("row")
    n_col = lax.axis_size("col")
    row, col = lax.axis_index("row"), lax.axis_index("col")
    images = n_col // n_row
    inner = b_panels.shape[0] // images
    count_blocks = owner_block.size
    capacity = max(2, (2 * count_blocks + n_row * n_col - 1) // (n_row * n_col))
    order = visit_order(n_row)
    every_row = list(range(n_row))
    early = list(range(TICKS - 1))
    backward = [((c + 1) % n_col, c) for c in range(n_col)]

    def image(number, part):
        depth = inner // PARTS
        start = (row + col + number * n_row) % n_col // n_row * inner + part * depth
        present = lax.dynamic_slice_in_dim(b_occupancy, start // BLK, depth // BLK, 0)
        return widen(present, lax.dynamic_slice_in_dim(b_panels, start, depth, 0))

    held = {("A", 0, 0): widen(a_occupancy, a_panels)}
    for part in range(PARTS):
        held["Y", part, 0] = image(1, part)
        held["X", part, 0] = image(0, part)
    mine = jnp.stack([owner_device.reshape(-1), owner_block.reshape(-1)])
    held["owners"] = jnp.broadcast_to(mine, (n_row * n_col,) + mine.shape)

    reach = n_row - 1
    first = [(("A", 0, -d), ("A", 0, d)) for d in range(1, reach)]
    lower = [(("Y", part, -d), ("X", part, d)) for d in range(1, n_row) for part in range(PARTS)]
    steps = []
    for number in range(max(len(first), len(lower))):
        steps += first[number : number + 1] + lower[number : number + 1]
    for d in range(1, reach):
        steps += [(("C", part, -d), ("Y", part, d)) for part in range(PARTS)]
    steps = [((("C", key[1], 0), other) if key[::2] == ("Y", -reach) else (key, other)) for key, other in steps]
    ends = {keys[0]: number for number, keys in enumerate(steps)}

    def relay(key):
        kind, part, offset = key
        sources = early if kind == "Y" else every_row
        if kind == "C":
            lower = held.get(("C", part, offset + 1), held["X", part, 0])
            later = held.get(("C", part, offset + 2), held["X", part, 0])
            later = held["Y", part, 1 - reach] if offset == 0 else later
            pairs = [(r, r + 1) for r in range(n_row - 1) if r == reach - 1 or -offset < reach - 1]
            return lax.ppermute(jnp.where(row == reach - 1, later, lower), "row", pairs)
        if offset < 0:
            return up_step(held[kind, part, offset + 1], sources, -offset, n_row)
        if kind == "Y" and offset > TICKS - 3:
            return None
        return down_step(held[kind, part, offset - 1], sources, offset)

    def close(due):
        held.update(due)
        held.update(zip(list(held), lax.optimization_barrier(tuple(held.values()))))

    def working(step):
        return [min(max(r, 1), n_row - 2) if step == n_row - 1 else r for r in range(n_row)]

    def chosen(step):
        offsets = [order[r][step] - r for r in working(step)]
        kinds = sorted(set(offsets))
        index = jnp.asarray([kinds.index(o) for o in offsets], jnp.int32)[row]
        cases = [held["A", 0, k] for k in kinds]
        return lax.select_n(index if len(cases) > 2 else index == 1, *cases)

    def product(step):
        keys = [
            [image_key(r, order[r][step] + t, n_row) for t in range(TICKS)] for r in working(step)
        ]
        names = sorted({key for of_row in keys for key in of_row})
        choices = [
            {t for r in range(n_row) for t in range(TICKS) if keys[r][t] == name} for name in names
        ]
        index = [[names.index(key) for key in of_row] for of_row in keys]
        which = jnp.asarray(index, jnp.int32)[row]
        last = step == n_row - 1
        of_step = ["last sent", "last full", "last used"] if last else ["sent", "full", "used"]
        return products(
            [held[name][0 if last else step] for name in of_step],
            which,
            [held["own" if step == 0 else "rest", t] for t in range(TICKS)],
            [[held[kind, part, offset] for part in range(PARTS)] for kind, offset in names],
            choices,
            max(step - 1, 0),
            4 if last else 1,
        )

    def exchange(step, blocks, total):
        targets, leader = held["got"][step], held["leader"][step]
        arrived = lax.all_to_all(blocks, "col", split_axis=0, concat_axis=0, tiled=True)
        if step == 0:
            return first_blocks(targets, arrived, total)
        return add_blocks(targets, leader, arrived, total)

    held["own", 0] = held["A", 0, 0][None]
    start_of = {ends["C", PARTS - 1, -step] + 2: step for step in range(reach)}
    last_number = ends["C", PARTS - 1, 2 - reach] + 2
    total = c_previous.reshape(c_previous.shape[2:])
    exchange_at = {at + (1 if step < reach - 2 else 2): step for at, step in start_of.items()}
    beside = [(1, 0), (n_row - 2, n_row - 1)]
    flying = {number: {} for number in range(2, 7)}
    for number in range(len(steps) + 2):
        if number >= 2:
            close(flying.pop(number))
        if number == last_number + 1:
            flying[len(steps) + 2] = {"half": lax.ppermute(held["side", 2], "row", beside)}
        step = exchange_at.get(number)
        if step is not None:
            total = exchange(step, held["blocks", step], total)
        if number < len(steps):
            moving = {key: relay(key) for key in steps[number]}
            flying.setdefault(number + 2, {}).update(
                {key: value for key, value in moving.items() if value is not None}
            )
        for name in ("own", "rest"):
            if name == "rest" and number == ends["A", 0, 1 - reach] + 2:
                held["rest", 0] = jnp.stack([chosen(step) for step in range(1, n_row)])
            ahead = [t for t in range(1, TICKS) if (name, t) not in held]
            if ahead and (name, ahead[0] - 1) in held and not any(
                (name, ahead[0]) in of_step for of_step in flying.values()
            ):
                hop = held[name, ahead[0] - 1]
                for t in ahead[: 2 if number == 0 else 1]:
                    hop = lax.ppermute(hop, "col", backward)
                    flying.setdefault(number + 2, {})[name, t] = hop
        if number == 2:
            every = lax.all_to_all(held["owners"], ("row", "col"), 0, 0, tiled=True)
            flying[5]["every"] = every
        if number == 5:
            flying[number + 1].update(tables(held["every"], n_row, n_col, capacity, order))
        if number in start_of and number < len(steps) + 1:
            (blocks,) = product(start_of[number])
            flying.setdefault(number + 1, {})["blocks", start_of[number]] = blocks
        if number == last_number:
            sides = product(n_row - 1)
            flying.setdefault(number + 1, {}).update({("side", k): v for k, v in enumerate(sides)})
    (blocks,) = product(n_row - 2)
    close({"blocks": blocks, **flying.pop(len(steps) + 2)})
    far = [held["half"], lax.ppermute(held["side", 3], "row", beside)]
    total = exchange(n_row - 2, held["blocks"], total)
    edge = (row == 0) | (row == n_row - 1)
    blocks = jnp.concatenate([jnp.where(edge, far[k], held["side", k]) for k in range(2)])
    total = exchange(n_row - 1, blocks, total)
    return total.reshape(c_previous.shape)


def solution(mesh):
    in_specs = (
        P("row", "col"),
        P("row", "col"),
        P("row", "col"),
        P("row", "col"),
        P("row", "col", None, None),
        P("row", "col", None),
        P("row", "col", None, None, None),
    )
    out_specs = P("row", "col", None, None, None)
    return jax.shard_map(
        per_device, mesh=mesh, in_specs=in_specs, out_specs=out_specs, check_vma=False
    )
```

```python
import functools

import jax
import jax.numpy as jnp
import numpy as np
from jax import lax
from jax.experimental import pallas as pl
from jax.experimental.pallas import tpu as pltpu
from jax.sharding import PartitionSpec as P

BLK = 128
TICKS = 4
PARTS = 2
ABREAST = 8
VMEM_LIMIT = 48 * 1024 * 1024


def widen(occupancy, panel):
    return panel * jnp.repeat(jnp.repeat(occupancy.astype(jnp.float32), BLK, axis=0), BLK, axis=1)


def up_step(value, sources, step, n_row):
    pairs = [(b + step - 1, b + step) for b in sources if b + step < n_row]
    return lax.ppermute(value, "row", pairs) if pairs else None


def down_step(value, sources, step):
    pairs = [(b - step + 1, b - step) for b in sources if b - step >= 0]
    return lax.ppermute(value, "row", pairs) if pairs else None


def visit_order(n_row):
    return [sorted(range(n_row), key=lambda i: (abs(i - r), i < r)) for r in range(n_row)]


def image_key(row, inner, n_row):
    source, kind = inner % n_row, "XY"[inner // n_row]
    last = n_row - 1
    if kind == "X" and source < row:
        return ("C", source - row + (row < last))
    if kind == "Y" and source - row == -last:
        return ("C", 0)
    return (kind, source - row)


def split(value):
    high = value.astype(jnp.bfloat16)
    low = (value - high.astype(jnp.float32)).astype(jnp.bfloat16)
    return high, low


def product_kernel(place, choices, pieces, table, full, used, which, *refs):
    count = len(choices) * PARTS
    lefts = refs[:TICKS]
    rights = refs[TICKS : TICKS + count]
    outs = refs[TICKS + count : TICKS + count + pieces]
    left_in, right_in, left_two, right_two, out, left_sem, right_sem, out_sem = refs[TICKS + count + pieces :]
    inner = right_in.shape[1]
    q_blocks = right_in.shape[2] // BLK

    def left_copy(t):
        return pltpu.make_async_copy(lefts[t].at[place], left_in.at[t], left_sem.at[t])

    for t in range(TICKS):
        left_copy(t).start()
        for position, ticks in enumerate(choices):
            of_image = rights[position * PARTS : (position + 1) * PARTS]
            if t in ticks:

                @pl.when(which[t] == position)
                def _():
                    for part, ref in enumerate(of_image):
                        rows = pl.ds(part * ref.shape[0], ref.shape[0])
                        pltpu.make_async_copy(ref, right_in.at[t, rows], right_sem.at[t]).start()

    for t in range(TICKS):
        left_copy(t).wait()
        pltpu.make_async_copy(right_in.at[t], right_in.at[t], right_sem.at[t]).wait()
        cols = pl.ds(t * inner, inner)

        @pl.loop(0, left_in.shape[1] // BLK)
        def _(p):
            rows = pl.ds(pl.multiple_of(p * BLK, BLK), BLK)
            high, low = split(left_in[t, rows, :])
            left_two[pl.ds(pl.multiple_of(p * 2 * BLK, 2 * BLK), BLK), cols] = high
            left_two[pl.ds(pl.multiple_of(p * 2 * BLK + BLK, BLK), BLK), cols] = low

        @pl.loop(0, inner // 32)
        def _(p):
            rows = pl.ds(pl.multiple_of(p * 32, 32), 32)
            to = pl.ds(pl.multiple_of(t * inner + p * 32, 32), 32)
            for q in range(q_blocks):
                high, low = split(right_in[t, rows, q * BLK : (q + 1) * BLK])
                right_two[to, 2 * q * BLK : (2 * q + 1) * BLK] = high
                right_two[to, (2 * q + 1) * BLK : (2 * q + 2) * BLK] = low

    def one(slot):
        block = jnp.maximum(table[slot], 0)
        rows = pl.ds(pl.multiple_of((block // q_blocks) * 2 * BLK, 2 * BLK), 2 * BLK)
        cols = pl.ds(pl.multiple_of((block % q_blocks) * 2 * BLK, 2 * BLK), 2 * BLK)
        four = jnp.dot(left_two[rows, :], right_two[:, cols], preferred_element_type=jnp.float32)
        out[slot] = (four[:BLK, :BLK] + (four[:BLK, BLK:] + four[BLK:, :BLK])) + four[BLK:, BLK:]

    @pl.loop(0, (used[0] + ABREAST - 1) // ABREAST)
    def _(turn):
        for extra in range(ABREAST):
            one(full[turn * ABREAST + extra])

    copies = []
    for piece, ref in enumerate(outs):
        slots = pl.ds(piece * ref.shape[0], ref.shape[0])
        copies.append(pltpu.make_async_copy(out.at[slots], ref, out_sem.at[piece]))
        copies[-1].start()
    for copy in copies:
        copy.wait()


def products(slots_used, which, lefts, rights, choices, place, pieces):
    rows, inner = lefts[0].shape[-2:]
    cols = rights[0][0].shape[1]
    rights = [part for of_image in rights for part in of_image]
    smem = pl.BlockSpec(memory_space=pltpu.SMEM)
    hbm = pl.BlockSpec(memory_space=pl.ANY)
    deep = TICKS * inner
    slots = slots_used[0].shape[0]
    return pl.pallas_call(
        functools.partial(product_kernel, place, choices, pieces),
        out_shape=[jax.ShapeDtypeStruct((slots // pieces, BLK, BLK), jnp.float32)] * pieces,
        in_specs=[smem] * 4 + [hbm] * (TICKS + len(rights)),
        out_specs=[hbm] * pieces,
        scratch_shapes=[
            pltpu.VMEM((TICKS, rows, inner), jnp.float32),
            pltpu.VMEM((TICKS, inner, cols), jnp.float32),
            pltpu.VMEM((2 * rows, deep), jnp.bfloat16),
            pltpu.VMEM((deep, 2 * cols), jnp.bfloat16),
            pltpu.VMEM((slots, BLK, BLK), jnp.float32),
            pltpu.SemaphoreType.DMA((TICKS,)),
            pltpu.SemaphoreType.DMA((TICKS,)),
            pltpu.SemaphoreType.DMA((pieces,)),
        ],
        compiler_params=pltpu.CompilerParams(vmem_limit_bytes=VMEM_LIMIT),
        cost_estimate=pl.CostEstimate(
            flops=2 * 6 * slots * BLK * BLK * deep,
            bytes_accessed=4 * (deep * (rows + cols) + slots * BLK * BLK),
            transcendentals=0,
        ),
        name="products",
    )(*slots_used, which, *lefts, *rights)


def add_kernel(targets, leader, got, start, out, got_in, total, got_sem, start_sem, out_sem):
    slots = got.shape[0]

    def got_copy(slot):
        return pltpu.make_async_copy(got.at[slot], got_in.at[slot], got_sem.at[slot])

    def start_copy(slot):
        return pltpu.make_async_copy(out.at[targets[slot]], total.at[slot], start_sem.at[slot])

    def out_copy(slot):
        return pltpu.make_async_copy(total.at[slot], out.at[targets[slot]], out_sem.at[slot])

    def every(leads, work):
        @pl.loop(0, slots)
        def _(slot):
            there = targets[slot] >= 0
            if leads:
                there = jnp.logical_and(there, leader[slot] == slot)

            @pl.when(there)
            def _():
                work(slot)

    every(True, lambda slot: start_copy(slot).start())
    every(False, lambda slot: got_copy(slot).start())
    every(True, lambda slot: start_copy(slot).wait())

    def add(slot):
        got_copy(slot).wait()
        total[leader[slot]] = total[leader[slot]] + got_in[slot]

    every(False, add)
    every(True, lambda slot: out_copy(slot).start())
    every(True, lambda slot: out_copy(slot).wait())


def add_blocks(targets, leader, got, start):
    smem = pl.BlockSpec(memory_space=pltpu.SMEM)
    hbm = pl.BlockSpec(memory_space=pl.ANY)
    slots = got.shape[0]
    return pl.pallas_call(
        add_kernel,
        out_shape=jax.ShapeDtypeStruct(start.shape, jnp.float32),
        in_specs=[smem, smem, hbm, hbm],
        out_specs=hbm,
        input_output_aliases={3: 0},
        scratch_shapes=[
            pltpu.VMEM(got.shape, jnp.float32),
            pltpu.VMEM(got.shape, jnp.float32),
            pltpu.SemaphoreType.DMA((slots,)),
            pltpu.SemaphoreType.DMA((slots,)),
            pltpu.SemaphoreType.DMA((slots,)),
        ],
        compiler_params=pltpu.CompilerParams(vmem_limit_bytes=VMEM_LIMIT),
        cost_estimate=pl.CostEstimate(
            flops=got.size, bytes_accessed=4 * 3 * got.size, transcendentals=0
        ),
        name="add_blocks",
    )(targets, leader, got, start)


def first_kernel(targets, got, start, out):
    out[...] = start[...]

    @pl.loop(0, got.shape[0])
    def _(slot):
        target = targets[slot]

        @pl.when(target >= 0)
        def _():
            out[target] = out[target] + got[slot]


def first_blocks(targets, got, start):
    vmem = pl.BlockSpec(memory_space=pltpu.VMEM)
    return pl.pallas_call(
        first_kernel,
        out_shape=jax.ShapeDtypeStruct(start.shape, jnp.float32),
        in_specs=[pl.BlockSpec(memory_space=pltpu.SMEM), vmem, vmem],
        out_specs=vmem,
        compiler_params=pltpu.CompilerParams(vmem_limit_bytes=VMEM_LIMIT),
        cost_estimate=pl.CostEstimate(
            flops=got.size, bytes_accessed=4 * (got.size + 2 * start.size), transcendentals=0
        ),
        name="first_blocks",
    )(targets, got, start)


def tables(every, n_row, n_col, capacity, order):
    row, col = lax.axis_index("row"), lax.axis_index("col")
    count = every.shape[-1]
    every = every.reshape(n_row, n_col, 2, count)
    places = jnp.arange(capacity, dtype=jnp.int32)
    columns = jnp.arange(n_col, dtype=jnp.int32)
    visits = jnp.asarray(order, jnp.int32)[row]

    def spread(match, values):
        rank = jnp.cumsum(match.astype(jnp.int32), axis=-1) - 1
        hit = match[..., None, :] & (rank[..., None, :] == places[:, None])
        return jnp.max(jnp.where(hit, values[..., None, :], -1), axis=-1)

    column = lax.dynamic_index_in_dim(every[:, :, 0], col, axis=1, keepdims=False)[visits]
    numbers = jnp.arange(count, dtype=jnp.int32)

    def slots_of(blocks, owners):
        match = blocks[:, None, :] == owners[..., None]
        return spread(match, jnp.broadcast_to(numbers, match.shape)).reshape(len(blocks), -1)

    def listed(sent):
        there = (sent >= 0).astype(jnp.int32)
        used = jnp.sum(there, axis=-1, keepdims=True)
        rank = jnp.cumsum(there, axis=-1)
        wanted = jnp.minimum(jnp.arange(sent.shape[-1], dtype=jnp.int32) + 1, used)
        full = jnp.argmax(rank[:, None, :] >= wanted[..., None], axis=-1).astype(jnp.int32)
        return sent, full, used

    sent = listed(slots_of(column[:-1], jnp.broadcast_to(row * n_col + columns, (n_row - 1, n_col))))
    beside = jnp.where(row == 1, 0, jnp.where(row == n_row - 2, n_row - 1, -1))
    inside = jnp.where((row == 0) | (row == n_row - 1), -1, row)
    rows = jnp.stack([inside, beside])
    owners = jnp.where(rows[:, None] >= 0, rows[:, None] * n_col + columns, -1)
    final = listed(slots_of(column[-1:], owners.reshape(1, -1)))

    arriving = every[visits]
    got = spread(arriving[:, :, 0] == row * n_col + col, arriving[:, :, 1])
    got = got.reshape(n_row, n_col * capacity)
    leader = jnp.argmax(got[:, :, None] == got[:, None, :], axis=-1).astype(jnp.int32)
    names = ("sent", "full", "used", "last sent", "last full", "last used", "got", "leader")
    return dict(zip(names, (*sent, *final, got, leader)))


def per_device(a_panels, b_panels, a_occupancy, b_occupancy, owner_device, owner_block, c_previous):
    n_row = lax.axis_size("row")
    n_col = lax.axis_size("col")
    row, col = lax.axis_index("row"), lax.axis_index("col")
    images = n_col // n_row
    inner = b_panels.shape[0] // images
    count_blocks = owner_block.size
    capacity = max(2, (2 * count_blocks + n_row * n_col - 1) // (n_row * n_col))
    order = visit_order(n_row)
    every_row = list(range(n_row))
    early = list(range(TICKS - 1))
    backward = [((c + 1) % n_col, c) for c in range(n_col)]

    def image(number, part):
        depth = inner // PARTS
        start = (row + col + number * n_row) % n_col // n_row * inner + part * depth
        present = lax.dynamic_slice_in_dim(b_occupancy, start // BLK, depth // BLK, 0)
        return widen(present, lax.dynamic_slice_in_dim(b_panels, start, depth, 0))

    held = {("A", 0, 0): widen(a_occupancy, a_panels)}
    for part in range(PARTS):
        held["Y", part, 0] = image(1, part)
        held["X", part, 0] = image(0, part)
    mine = jnp.stack([owner_device.reshape(-1), owner_block.reshape(-1)])
    held["owners"] = jnp.broadcast_to(mine, (n_row * n_col,) + mine.shape)

    reach = n_row - 1
    first = [(("A", 0, -d), ("A", 0, d)) for d in range(1, reach)]
    lower = [(("Y", part, -d), ("X", part, d)) for d in range(1, n_row) for part in range(PARTS)]
    steps = []
    for number in range(max(len(first), len(lower))):
        steps += first[number : number + 1] + lower[number : number + 1]
    for d in range(1, reach):
        steps += [(("C", part, -d), ("Y", part, d)) for part in range(PARTS)]
    steps = [((("C", key[1], 0), other) if key[::2] == ("Y", -reach) else (key, other)) for key, other in steps]
    ends = {keys[0]: number for number, keys in enumerate(steps)}

    def relay(key):
        kind, part, offset = key
        sources = early if kind == "Y" else every_row
        if kind == "C":
            lower = held.get(("C", part, offset + 1), held["X", part, 0])
            later = held.get(("C", part, offset + 2), held["X", part, 0])
            later = held["Y", part, 1 - reach] if offset == 0 else later
            pairs = [(r, r + 1) for r in range(n_row - 1) if r == reach - 1 or -offset < reach - 1]
            return lax.ppermute(jnp.where(row == reach - 1, later, lower), "row", pairs)
        if offset < 0:
            return up_step(held[kind, part, offset + 1], sources, -offset, n_row)
        if kind == "Y" and offset > TICKS - 3:
            return None
        return down_step(held[kind, part, offset - 1], sources, offset)

    def close(due):
        held.update(due)
        held.update(zip(list(held), lax.optimization_barrier(tuple(held.values()))))

    def hops(name, panels):
        found = {(name, 0): panels}
        for t in range(1, TICKS):
            found[name, t] = lax.ppermute(found[name, t - 1], "col", backward)
        return found

    def working(step):
        return [min(max(r, 1), n_row - 2) if step == n_row - 1 else r for r in range(n_row)]

    def chosen(step):
        offsets = [order[r][step] - r for r in working(step)]
        kinds = sorted(set(offsets))
        index = jnp.asarray([kinds.index(o) for o in offsets], jnp.int32)[row]
        cases = [held["A", 0, k] for k in kinds]
        return lax.select_n(index if len(cases) > 2 else index == 1, *cases)

    def product(step):
        keys = [
            [image_key(r, order[r][step] + t, n_row) for t in range(TICKS)] for r in working(step)
        ]
        names = sorted({key for of_row in keys for key in of_row})
        choices = [
            {t for r in range(n_row) for t in range(TICKS) if keys[r][t] == name} for name in names
        ]
        index = [[names.index(key) for key in of_row] for of_row in keys]
        which = jnp.asarray(index, jnp.int32)[row]
        last = step == n_row - 1
        of_step = ["last sent", "last full", "last used"] if last else ["sent", "full", "used"]
        return products(
            [held[name][0 if last else step] for name in of_step],
            which,
            [held["own" if step == 0 else "rest", t] for t in range(TICKS)],
            [[held[kind, part, offset] for part in range(PARTS)] for kind, offset in names],
            choices,
            max(step - 1, 0),
            4 if last else 1,
        )

    def exchange(step, blocks, total):
        targets, leader = held["got"][step], held["leader"][step]
        arrived = lax.all_to_all(blocks, "col", split_axis=0, concat_axis=0, tiled=True)
        if step == 0:
            return first_blocks(targets, arrived, total)
        return add_blocks(targets, leader, arrived, total)

    start_of = {ends["C", PARTS - 1, -step] + 2: step for step in range(reach)}
    last_number = ends["C", PARTS - 1, 2 - reach] + 2
    total = c_previous.reshape(c_previous.shape[2:])
    exchange_at = {at + (1 if step < reach - 2 else 2): step for at, step in start_of.items()}
    beside = [(1, 0), (n_row - 2, n_row - 1)]
    flying = {number: {} for number in range(2, 11)}
    for number in range(len(steps) + 2):
        if number >= 2:
            close(flying.pop(number, {}))
        if number == last_number + 1:
            flying[len(steps) + 2] = {"half": lax.ppermute(held["side", 2], "row", beside)}
        step = exchange_at.get(number)
        if step is not None:
            total = exchange(step, held["blocks", step], total)
        if number < len(steps):
            moving = {key: relay(key) for key in steps[number]}
            flying.setdefault(number + 2, {}).update(
                {key: value for key, value in moving.items() if value is not None}
            )
        if number == 0:
            flying[3].update(hops("own", held["A", 0, 0][None]))
        if number == ends["A", 0, 1 - reach] + 2:
            panels = jnp.stack([chosen(step) for step in range(1, n_row)])
            flying.setdefault(number + 6, {}).update(hops("rest", panels))
        if number == 2:
            every = lax.all_to_all(held["owners"], ("row", "col"), 0, 0, tiled=True)
            flying[5]["every"] = every
        if number == 5:
            flying[number + 1].update(tables(held["every"], n_row, n_col, capacity, order))
        if number in start_of and number < len(steps) + 1:
            (blocks,) = product(start_of[number])
            flying.setdefault(number + 1, {})["blocks", start_of[number]] = blocks
        if number == last_number:
            sides = product(n_row - 1)
            flying.setdefault(number + 1, {}).update({("side", k): v for k, v in enumerate(sides)})
    (blocks,) = product(n_row - 2)
    close({"blocks": blocks, **flying.pop(len(steps) + 2)})
    far = [held["half"], lax.ppermute(held["side", 3], "row", beside)]
    total = exchange(n_row - 2, held["blocks"], total)
    edge = (row == 0) | (row == n_row - 1)
    blocks = jnp.concatenate([jnp.where(edge, far[k], held["side", k]) for k in range(2)])
    total = exchange(n_row - 1, blocks, total)
    return total.reshape(c_previous.shape)


def solution(mesh):
    in_specs = (
        P("row", "col"),
        P("row", "col"),
        P("row", "col"),
        P("row", "col"),
        P("row", "col", None, None),
        P("row", "col", None),
        P("row", "col", None, None, None),
    )
    out_specs = P("row", "col", None, None, None)
    return jax.shard_map(
        per_device, mesh=mesh, in_specs=in_specs, out_specs=out_specs, check_vma=False
    )
```

```python
import functools

import jax
import jax.numpy as jnp
import numpy as np
from jax import lax
from jax.experimental import pallas as pl
from jax.experimental.pallas import tpu as pltpu
from jax.sharding import PartitionSpec as P

BLK = 128
TICKS = 4
PARTS = 2
ABREAST = 8
VMEM_LIMIT = 48 * 1024 * 1024


def widen(occupancy, panel):
    return panel * jnp.repeat(jnp.repeat(occupancy.astype(jnp.float32), BLK, axis=0), BLK, axis=1)


def up_step(value, sources, step, n_row):
    pairs = [(b + step - 1, b + step) for b in sources if b + step < n_row]
    return lax.ppermute(value, "row", pairs) if pairs else None


def down_step(value, sources, step):
    pairs = [(b - step + 1, b - step) for b in sources if b - step >= 0]
    return lax.ppermute(value, "row", pairs) if pairs else None


def visit_order(n_row):
    return [sorted(range(n_row), key=lambda i: (abs(i - r), i < r)) for r in range(n_row)]


def image_key(row, inner, n_row):
    source, kind = inner % n_row, "XY"[inner // n_row]
    last = n_row - 1
    if kind == "X" and source < row:
        return ("C", source - row + (row < last))
    if kind == "Y" and source - row == -last:
        return ("C", 0)
    return (kind, source - row)


def split(value):
    high = value.astype(jnp.bfloat16)
    low = (value - high.astype(jnp.float32)).astype(jnp.bfloat16)
    return high, low


def product_kernel(place, choices, pieces, table, full, used, which, *refs):
    count = len(choices) * PARTS
    lefts = refs[:TICKS]
    rights = refs[TICKS : TICKS + count]
    outs = refs[TICKS + count : TICKS + count + pieces]
    left_in, right_in, left_two, right_two, out, left_sem, right_sem, out_sem = refs[TICKS + count + pieces :]
    inner = right_in.shape[1]
    q_blocks = right_in.shape[2] // BLK

    def left_copy(t):
        return pltpu.make_async_copy(lefts[t].at[place], left_in.at[t], left_sem.at[t])

    for t in range(TICKS):
        left_copy(t).start()
        for position, ticks in enumerate(choices):
            of_image = rights[position * PARTS : (position + 1) * PARTS]
            if t in ticks:

                @pl.when(which[t] == position)
                def _():
                    for part, ref in enumerate(of_image):
                        rows = pl.ds(part * ref.shape[0], ref.shape[0])
                        pltpu.make_async_copy(ref, right_in.at[t, rows], right_sem.at[t]).start()

    for t in range(TICKS):
        left_copy(t).wait()
        pltpu.make_async_copy(right_in.at[t], right_in.at[t], right_sem.at[t]).wait()
        cols = pl.ds(t * inner, inner)

        @pl.loop(0, left_in.shape[1] // BLK)
        def _(p):
            rows = pl.ds(pl.multiple_of(p * BLK, BLK), BLK)
            high, low = split(left_in[t, rows, :])
            left_two[pl.ds(pl.multiple_of(p * 2 * BLK, 2 * BLK), BLK), cols] = high
            left_two[pl.ds(pl.multiple_of(p * 2 * BLK + BLK, BLK), BLK), cols] = low

        @pl.loop(0, inner // 32)
        def _(p):
            rows = pl.ds(pl.multiple_of(p * 32, 32), 32)
            to = pl.ds(pl.multiple_of(t * inner + p * 32, 32), 32)
            for q in range(q_blocks):
                high, low = split(right_in[t, rows, q * BLK : (q + 1) * BLK])
                right_two[to, 2 * q * BLK : (2 * q + 1) * BLK] = high
                right_two[to, (2 * q + 1) * BLK : (2 * q + 2) * BLK] = low

    def one(slot):
        block = jnp.maximum(table[slot], 0)
        rows = pl.ds(pl.multiple_of((block // q_blocks) * 2 * BLK, 2 * BLK), 2 * BLK)
        cols = pl.ds(pl.multiple_of((block % q_blocks) * 2 * BLK, 2 * BLK), 2 * BLK)
        four = jnp.dot(left_two[rows, :], right_two[:, cols], preferred_element_type=jnp.float32)
        out[slot] = (four[:BLK, :BLK] + (four[:BLK, BLK:] + four[BLK:, :BLK])) + four[BLK:, BLK:]

    @pl.loop(0, (used[0] + ABREAST - 1) // ABREAST)
    def _(turn):
        for extra in range(ABREAST):
            one(full[turn * ABREAST + extra])

    copies = []
    for piece, ref in enumerate(outs):
        slots = pl.ds(piece * ref.shape[0], ref.shape[0])
        copies.append(pltpu.make_async_copy(out.at[slots], ref, out_sem.at[piece]))
        copies[-1].start()
    for copy in copies:
        copy.wait()


def products(slots_used, which, lefts, rights, choices, place, pieces):
    rows, inner = lefts[0].shape[-2:]
    cols = rights[0][0].shape[1]
    rights = [part for of_image in rights for part in of_image]
    smem = pl.BlockSpec(memory_space=pltpu.SMEM)
    hbm = pl.BlockSpec(memory_space=pl.ANY)
    deep = TICKS * inner
    slots = slots_used[0].shape[0]
    return pl.pallas_call(
        functools.partial(product_kernel, place, choices, pieces),
        out_shape=[jax.ShapeDtypeStruct((slots // pieces, BLK, BLK), jnp.float32)] * pieces,
        in_specs=[smem] * 4 + [hbm] * (TICKS + len(rights)),
        out_specs=[hbm] * pieces,
        scratch_shapes=[
            pltpu.VMEM((TICKS, rows, inner), jnp.float32),
            pltpu.VMEM((TICKS, inner, cols), jnp.float32),
            pltpu.VMEM((2 * rows, deep), jnp.bfloat16),
            pltpu.VMEM((deep, 2 * cols), jnp.bfloat16),
            pltpu.VMEM((slots, BLK, BLK), jnp.float32),
            pltpu.SemaphoreType.DMA((TICKS,)),
            pltpu.SemaphoreType.DMA((TICKS,)),
            pltpu.SemaphoreType.DMA((pieces,)),
        ],
        compiler_params=pltpu.CompilerParams(vmem_limit_bytes=VMEM_LIMIT),
        cost_estimate=pl.CostEstimate(
            flops=2 * 6 * slots * BLK * BLK * deep,
            bytes_accessed=4 * (deep * (rows + cols) + slots * BLK * BLK),
            transcendentals=0,
        ),
        name="products",
    )(*slots_used, which, *lefts, *rights)


def add_kernel(targets, leader, got, start, out, got_in, total, got_sem, start_sem, out_sem):
    slots = got.shape[0]

    def got_copy(slot):
        return pltpu.make_async_copy(got.at[slot], got_in.at[slot], got_sem.at[slot])

    def start_copy(slot):
        return pltpu.make_async_copy(out.at[targets[slot]], total.at[slot], start_sem.at[slot])

    def out_copy(slot):
        return pltpu.make_async_copy(total.at[slot], out.at[targets[slot]], out_sem.at[slot])

    def every(leads, work):
        @pl.loop(0, slots)
        def _(slot):
            there = targets[slot] >= 0
            if leads:
                there = jnp.logical_and(there, leader[slot] == slot)

            @pl.when(there)
            def _():
                work(slot)

    every(True, lambda slot: start_copy(slot).start())
    every(False, lambda slot: got_copy(slot).start())
    every(True, lambda slot: start_copy(slot).wait())

    def add(slot):
        got_copy(slot).wait()
        total[leader[slot]] = total[leader[slot]] + got_in[slot]

    every(False, add)
    every(True, lambda slot: out_copy(slot).start())
    every(True, lambda slot: out_copy(slot).wait())


def add_blocks(targets, leader, got, start):
    smem = pl.BlockSpec(memory_space=pltpu.SMEM)
    hbm = pl.BlockSpec(memory_space=pl.ANY)
    slots = got.shape[0]
    return pl.pallas_call(
        add_kernel,
        out_shape=jax.ShapeDtypeStruct(start.shape, jnp.float32),
        in_specs=[smem, smem, hbm, hbm],
        out_specs=hbm,
        input_output_aliases={3: 0},
        scratch_shapes=[
            pltpu.VMEM(got.shape, jnp.float32),
            pltpu.VMEM(got.shape, jnp.float32),
            pltpu.SemaphoreType.DMA((slots,)),
            pltpu.SemaphoreType.DMA((slots,)),
            pltpu.SemaphoreType.DMA((slots,)),
        ],
        compiler_params=pltpu.CompilerParams(vmem_limit_bytes=VMEM_LIMIT),
        cost_estimate=pl.CostEstimate(
            flops=got.size, bytes_accessed=4 * 3 * got.size, transcendentals=0
        ),
        name="add_blocks",
    )(targets, leader, got, start)


def first_kernel(targets, got, start, out):
    out[...] = start[...]

    @pl.loop(0, got.shape[0])
    def _(slot):
        target = targets[slot]

        @pl.when(target >= 0)
        def _():
            out[target] = out[target] + got[slot]


def first_blocks(targets, got, start):
    vmem = pl.BlockSpec(memory_space=pltpu.VMEM)
    return pl.pallas_call(
        first_kernel,
        out_shape=jax.ShapeDtypeStruct(start.shape, jnp.float32),
        in_specs=[pl.BlockSpec(memory_space=pltpu.SMEM), vmem, vmem],
        out_specs=vmem,
        compiler_params=pltpu.CompilerParams(vmem_limit_bytes=VMEM_LIMIT),
        cost_estimate=pl.CostEstimate(
            flops=got.size, bytes_accessed=4 * (got.size + 2 * start.size), transcendentals=0
        ),
        name="first_blocks",
    )(targets, got, start)


def tables(every, n_row, n_col, capacity, order):
    row, col = lax.axis_index("row"), lax.axis_index("col")
    count = every.shape[-1]
    every = every.reshape(n_row, n_col, 2, count)
    places = jnp.arange(capacity, dtype=jnp.int32)
    columns = jnp.arange(n_col, dtype=jnp.int32)
    visits = jnp.asarray(order, jnp.int32)[row]

    def spread(match, values):
        rank = jnp.cumsum(match.astype(jnp.int32), axis=-1) - 1
        hit = match[..., None, :] & (rank[..., None, :] == places[:, None])
        return jnp.max(jnp.where(hit, values[..., None, :], -1), axis=-1)

    column = lax.dynamic_index_in_dim(every[:, :, 0], col, axis=1, keepdims=False)[visits]
    numbers = jnp.arange(count, dtype=jnp.int32)

    def slots_of(blocks, owners):
        match = blocks[:, None, :] == owners[..., None]
        return spread(match, jnp.broadcast_to(numbers, match.shape)).reshape(len(blocks), -1)

    def listed(sent):
        there = (sent >= 0).astype(jnp.int32)
        used = jnp.sum(there, axis=-1, keepdims=True)
        rank = jnp.cumsum(there, axis=-1)
        wanted = jnp.minimum(jnp.arange(sent.shape[-1], dtype=jnp.int32) + 1, used)
        full = jnp.argmax(rank[:, None, :] >= wanted[..., None], axis=-1).astype(jnp.int32)
        return sent, full, used

    sent = listed(slots_of(column[:-1], jnp.broadcast_to(row * n_col + columns, (n_row - 1, n_col))))
    beside = jnp.where(row == 1, 0, jnp.where(row == n_row - 2, n_row - 1, -1))
    inside = jnp.where((row == 0) | (row == n_row - 1), -1, row)
    rows = jnp.stack([inside, beside])
    owners = jnp.where(rows[:, None] >= 0, rows[:, None] * n_col + columns, -1)
    final = listed(slots_of(column[-1:], owners.reshape(1, -1)))

    arriving = every[visits]
    got = spread(arriving[:, :, 0] == row * n_col + col, arriving[:, :, 1])
    got = got.reshape(n_row, n_col * capacity)
    leader = jnp.argmax(got[:, :, None] == got[:, None, :], axis=-1).astype(jnp.int32)
    names = ("sent", "full", "used", "last sent", "last full", "last used", "got", "leader")
    return dict(zip(names, (*sent, *final, got, leader)))


def per_device(a_panels, b_panels, a_occupancy, b_occupancy, owner_device, owner_block, c_previous):
    n_row = lax.axis_size("row")
    n_col = lax.axis_size("col")
    row, col = lax.axis_index("row"), lax.axis_index("col")
    images = n_col // n_row
    inner = b_panels.shape[0] // images
    count_blocks = owner_block.size
    capacity = max(2, (2 * count_blocks + n_row * n_col - 1) // (n_row * n_col))
    order = visit_order(n_row)
    every_row = list(range(n_row))
    early = list(range(TICKS - 1))
    backward = [((c + 1) % n_col, c) for c in range(n_col)]

    def image(number, part):
        depth = inner // PARTS
        start = (row + col + number * n_row) % n_col // n_row * inner + part * depth
        present = lax.dynamic_slice_in_dim(b_occupancy, start // BLK, depth // BLK, 0)
        return widen(present, lax.dynamic_slice_in_dim(b_panels, start, depth, 0))

    held = {("A", 0, 0): widen(a_occupancy, a_panels)}
    for part in range(PARTS):
        held["Y", part, 0] = image(1, part)
        held["X", part, 0] = image(0, part)
    mine = jnp.stack([owner_device.reshape(-1), owner_block.reshape(-1)])
    held["owners"] = jnp.broadcast_to(mine, (n_row * n_col,) + mine.shape)

    reach = n_row - 1
    first = [(("A", 0, -d), ("A", 0, d)) for d in range(1, reach)]
    lower = [(("Y", part, -d), ("X", part, d)) for d in range(1, n_row) for part in range(PARTS)]
    steps = []
    for number in range(max(len(first), len(lower))):
        steps += first[number : number + 1] + lower[number : number + 1]
    for d in range(1, reach):
        steps += [(("C", part, -d), ("Y", part, d)) for part in range(PARTS)]
    steps = [((("C", key[1], 0), other) if key[::2] == ("Y", -reach) else (key, other)) for key, other in steps]
    ends = {keys[0]: number for number, keys in enumerate(steps)}

    def relay(key):
        kind, part, offset = key
        sources = early if kind == "Y" else every_row
        if kind == "C":
            lower = held.get(("C", part, offset + 1), held["X", part, 0])
            later = held.get(("C", part, offset + 2), held["X", part, 0])
            later = held["Y", part, 1 - reach] if offset == 0 else later
            pairs = [(r, r + 1) for r in range(n_row - 1) if r == reach - 1 or -offset < reach - 1]
            return lax.ppermute(jnp.where(row == reach - 1, later, lower), "row", pairs)
        if offset < 0:
            return up_step(held[kind, part, offset + 1], sources, -offset, n_row)
        if kind == "Y" and offset > TICKS - 3:
            return None
        return down_step(held[kind, part, offset - 1], sources, offset)

    def close(due):
        held.update(due)
        held.update(zip(list(held), lax.optimization_barrier(tuple(held.values()))))

    def hops(name, panels):
        found = {(name, 0): panels}
        for t in range(1, TICKS):
            found[name, t] = lax.ppermute(found[name, t - 1], "col", backward)
        return found

    def working(step):
        return [min(max(r, 1), n_row - 2) if step == n_row - 1 else r for r in range(n_row)]

    def chosen(step):
        offsets = [order[r][step] - r for r in working(step)]
        kinds = sorted(set(offsets))
        index = jnp.asarray([kinds.index(o) for o in offsets], jnp.int32)[row]
        cases = [held["A", 0, k] for k in kinds]
        return lax.select_n(index if len(cases) > 2 else index == 1, *cases)

    def product(step):
        keys = [
            [image_key(r, order[r][step] + t, n_row) for t in range(TICKS)] for r in working(step)
        ]
        names = sorted({key for of_row in keys for key in of_row})
        choices = [
            {t for r in range(n_row) for t in range(TICKS) if keys[r][t] == name} for name in names
        ]
        index = [[names.index(key) for key in of_row] for of_row in keys]
        which = jnp.asarray(index, jnp.int32)[row]
        last = step == n_row - 1
        of_step = ["last sent", "last full", "last used"] if last else ["sent", "full", "used"]
        return products(
            [held[name][0 if last else step] for name in of_step],
            which,
            [held["own" if step == 0 else "rest", t] for t in range(TICKS)],
            [[held[kind, part, offset] for part in range(PARTS)] for kind, offset in names],
            choices,
            max(step - 1, 0),
            4 if last else 1,
        )

    def exchange(step, blocks, total):
        targets, leader = held["got"][step], held["leader"][step]
        arrived = lax.all_to_all(blocks, "col", split_axis=0, concat_axis=0, tiled=True)
        if step == 0:
            return first_blocks(targets, arrived, total)
        return add_blocks(targets, leader, arrived, total)

    start_of = {ends["C", PARTS - 1, -step] + 2: step for step in range(reach)}
    last_number = ends["C", PARTS - 1, 2 - reach] + 2
    total = c_previous.reshape(c_previous.shape[2:])
    exchange_at = {at + (1 if step < reach - 2 else 2): step for at, step in start_of.items()}
    beside = [(1, 0), (n_row - 2, n_row - 1)]
    flying = {number: {} for number in range(2, 11)}
    for number in range(len(steps) + 2):
        if number >= 2:
            close(flying.pop(number, {}))
        if number == last_number + 1:
            flying[len(steps) + 2] = {"half": lax.ppermute(held["side", 2], "row", beside)}
        step = exchange_at.get(number)
        if step is not None:
            total = exchange(step, held["blocks", step], total)
        if number < len(steps):
            moving = {key: relay(key) for key in steps[number]}
            flying.setdefault(number + 2, {}).update(
                {key: value for key, value in moving.items() if value is not None}
            )
        if number == 0:
            flying[3].update(hops("own", held["A", 0, 0][None]))
        if number == ends["A", 0, 1 - reach] + 2:
            panels = jnp.stack([chosen(step) for step in range(1, n_row)])
            flying.setdefault(number + 7, {}).update(hops("rest", panels))
        if number == 2:
            every = lax.all_to_all(held["owners"], ("row", "col"), 0, 0, tiled=True)
            flying[5]["every"] = every
        if number == 5:
            flying[number + 1].update(tables(held["every"], n_row, n_col, capacity, order))
        if number in start_of and number < len(steps) + 1:
            (blocks,) = product(start_of[number])
            flying.setdefault(number + 1, {})["blocks", start_of[number]] = blocks
        if number == last_number:
            sides = product(n_row - 1)
            flying.setdefault(number + 1, {}).update({("side", k): v for k, v in enumerate(sides)})
    (blocks,) = product(n_row - 2)
    close({"blocks": blocks, **flying.pop(len(steps) + 2)})
    far = [held["half"], lax.ppermute(held["side", 3], "row", beside)]
    total = exchange(n_row - 2, held["blocks"], total)
    edge = (row == 0) | (row == n_row - 1)
    blocks = jnp.concatenate([jnp.where(edge, far[k], held["side", k]) for k in range(2)])
    total = exchange(n_row - 1, blocks, total)
    return total.reshape(c_previous.shape)


def solution(mesh):
    in_specs = (
        P("row", "col"),
        P("row", "col"),
        P("row", "col"),
        P("row", "col"),
        P("row", "col", None, None),
        P("row", "col", None),
        P("row", "col", None, None, None),
    )
    out_specs = P("row", "col", None, None, None)
    return jax.shard_map(
        per_device, mesh=mesh, in_specs=in_specs, out_specs=out_specs, check_vma=False
    )
```

```python
import functools

import jax
import jax.numpy as jnp
import numpy as np
from jax import lax
from jax.experimental import pallas as pl
from jax.experimental.pallas import tpu as pltpu
from jax.sharding import PartitionSpec as P

BLK = 128
TICKS = 4
PARTS = 2
ABREAST = 8
VMEM_LIMIT = 48 * 1024 * 1024


def widen(occupancy, panel):
    return panel * jnp.repeat(jnp.repeat(occupancy.astype(jnp.float32), BLK, axis=0), BLK, axis=1)


def up_step(value, sources, step, n_row):
    pairs = [(b + step - 1, b + step) for b in sources if b + step < n_row]
    return lax.ppermute(value, "row", pairs) if pairs else None


def down_step(value, sources, step):
    pairs = [(b - step + 1, b - step) for b in sources if b - step >= 0]
    return lax.ppermute(value, "row", pairs) if pairs else None


def visit_order(n_row):
    return [sorted(range(n_row), key=lambda i: (abs(i - r), i < r)) for r in range(n_row)]


def image_key(row, inner, n_row):
    source, kind = inner % n_row, "XY"[inner // n_row]
    last = n_row - 1
    if kind == "X" and source < row:
        return ("C", source - row + (row < last))
    if kind == "Y" and source - row == -last:
        return ("C", 0)
    return (kind, source - row)


def split(value):
    high = value.astype(jnp.bfloat16)
    low = (value - high.astype(jnp.float32)).astype(jnp.bfloat16)
    return high, low


def product_kernel(place, choices, pieces, table, full, used, which, *refs):
    count = len(choices) * PARTS
    lefts = refs[:TICKS]
    rights = refs[TICKS : TICKS + count]
    outs = refs[TICKS + count : TICKS + count + pieces]
    left_in, right_in, left_two, right_two, out, left_sem, right_sem, out_sem = refs[TICKS + count + pieces :]
    inner = right_in.shape[1]
    q_blocks = right_in.shape[2] // BLK

    def left_copy(t):
        return pltpu.make_async_copy(lefts[t].at[place], left_in.at[t], left_sem.at[t])

    for t in range(TICKS):
        left_copy(t).start()
        for position, ticks in enumerate(choices):
            of_image = rights[position * PARTS : (position + 1) * PARTS]
            if t in ticks:

                @pl.when(which[t] == position)
                def _():
                    for part, ref in enumerate(of_image):
                        rows = pl.ds(part * ref.shape[0], ref.shape[0])
                        pltpu.make_async_copy(ref, right_in.at[t, rows], right_sem.at[t]).start()

    for t in range(TICKS):
        left_copy(t).wait()
        pltpu.make_async_copy(right_in.at[t], right_in.at[t], right_sem.at[t]).wait()
        cols = pl.ds(t * inner, inner)

        @pl.loop(0, left_in.shape[1] // BLK)
        def _(p):
            rows = pl.ds(pl.multiple_of(p * BLK, BLK), BLK)
            high, low = split(left_in[t, rows, :])
            left_two[pl.ds(pl.multiple_of(p * 2 * BLK, 2 * BLK), BLK), cols] = high
            left_two[pl.ds(pl.multiple_of(p * 2 * BLK + BLK, BLK), BLK), cols] = low

        @pl.loop(0, inner // 32)
        def _(p):
            rows = pl.ds(pl.multiple_of(p * 32, 32), 32)
            to = pl.ds(pl.multiple_of(t * inner + p * 32, 32), 32)
            for q in range(q_blocks):
                high, low = split(right_in[t, rows, q * BLK : (q + 1) * BLK])
                right_two[to, 2 * q * BLK : (2 * q + 1) * BLK] = high
                right_two[to, (2 * q + 1) * BLK : (2 * q + 2) * BLK] = low

    def one(slot):
        block = jnp.maximum(table[slot], 0)
        rows = pl.ds(pl.multiple_of((block // q_blocks) * 2 * BLK, 2 * BLK), 2 * BLK)
        cols = pl.ds(pl.multiple_of((block % q_blocks) * 2 * BLK, 2 * BLK), 2 * BLK)
        four = jnp.dot(left_two[rows, :], right_two[:, cols], preferred_element_type=jnp.float32)
        out[slot] = (four[:BLK, :BLK] + (four[:BLK, BLK:] + four[BLK:, :BLK])) + four[BLK:, BLK:]

    @pl.loop(0, (used[0] + ABREAST - 1) // ABREAST)
    def _(turn):
        for extra in range(ABREAST):
            one(full[turn * ABREAST + extra])

    copies = []
    for piece, ref in enumerate(outs):
        slots = pl.ds(piece * ref.shape[0], ref.shape[0])
        copies.append(pltpu.make_async_copy(out.at[slots], ref, out_sem.at[piece]))
        copies[-1].start()
    for copy in copies:
        copy.wait()


def products(slots_used, which, lefts, rights, choices, place, pieces):
    rows, inner = lefts[0].shape[-2:]
    cols = rights[0][0].shape[1]
    rights = [part for of_image in rights for part in of_image]
    smem = pl.BlockSpec(memory_space=pltpu.SMEM)
    hbm = pl.BlockSpec(memory_space=pl.ANY)
    deep = TICKS * inner
    slots = slots_used[0].shape[0]
    return pl.pallas_call(
        functools.partial(product_kernel, place, choices, pieces),
        out_shape=[jax.ShapeDtypeStruct((slots // pieces, BLK, BLK), jnp.float32)] * pieces,
        in_specs=[smem] * 4 + [hbm] * (TICKS + len(rights)),
        out_specs=[hbm] * pieces,
        scratch_shapes=[
            pltpu.VMEM((TICKS, rows, inner), jnp.float32),
            pltpu.VMEM((TICKS, inner, cols), jnp.float32),
            pltpu.VMEM((2 * rows, deep), jnp.bfloat16),
            pltpu.VMEM((deep, 2 * cols), jnp.bfloat16),
            pltpu.VMEM((slots, BLK, BLK), jnp.float32),
            pltpu.SemaphoreType.DMA((TICKS,)),
            pltpu.SemaphoreType.DMA((TICKS,)),
            pltpu.SemaphoreType.DMA((pieces,)),
        ],
        compiler_params=pltpu.CompilerParams(vmem_limit_bytes=VMEM_LIMIT),
        cost_estimate=pl.CostEstimate(
            flops=2 * 6 * slots * BLK * BLK * deep,
            bytes_accessed=4 * (deep * (rows + cols) + slots * BLK * BLK),
            transcendentals=0,
        ),
        name="products",
    )(*slots_used, which, *lefts, *rights)


def add_kernel(targets, leader, got, start, out, got_in, total, got_sem, start_sem, out_sem):
    slots = got.shape[0]

    def got_copy(slot):
        return pltpu.make_async_copy(got.at[slot], got_in.at[slot], got_sem.at[slot])

    def start_copy(slot):
        return pltpu.make_async_copy(out.at[targets[slot]], total.at[slot], start_sem.at[slot])

    def out_copy(slot):
        return pltpu.make_async_copy(total.at[slot], out.at[targets[slot]], out_sem.at[slot])

    def every(work):
        @pl.loop(0, slots)
        def _(slot):
            @pl.when(targets[slot] >= 0)
            def _():
                work(slot, leader[slot])

    def fetch(slot, lead):
        got_copy(slot).start()

        @pl.when(lead == slot)
        def _():
            start_copy(slot).start()

    def add(slot, lead):
        got_copy(slot).wait()

        @pl.when(lead == slot)
        def _():
            start_copy(slot).wait()

        total[lead] = total[lead] + got_in[slot]

    def store(slot, lead):
        @pl.when(lead == slot)
        def _():
            out_copy(slot).start()

    def stored(slot, lead):
        @pl.when(lead == slot)
        def _():
            out_copy(slot).wait()

    every(fetch)
    every(add)
    every(store)
    every(stored)


def add_blocks(targets, leader, got, start):
    smem = pl.BlockSpec(memory_space=pltpu.SMEM)
    hbm = pl.BlockSpec(memory_space=pl.ANY)
    slots = got.shape[0]
    return pl.pallas_call(
        add_kernel,
        out_shape=jax.ShapeDtypeStruct(start.shape, jnp.float32),
        in_specs=[smem, smem, hbm, hbm],
        out_specs=hbm,
        input_output_aliases={3: 0},
        scratch_shapes=[
            pltpu.VMEM(got.shape, jnp.float32),
            pltpu.VMEM(got.shape, jnp.float32),
            pltpu.SemaphoreType.DMA((slots,)),
            pltpu.SemaphoreType.DMA((slots,)),
            pltpu.SemaphoreType.DMA((slots,)),
        ],
        compiler_params=pltpu.CompilerParams(vmem_limit_bytes=VMEM_LIMIT),
        cost_estimate=pl.CostEstimate(
            flops=got.size, bytes_accessed=4 * 3 * got.size, transcendentals=0
        ),
        name="add_blocks",
    )(targets, leader, got, start)


def first_kernel(targets, got, start, out):
    out[...] = start[...]

    @pl.loop(0, got.shape[0])
    def _(slot):
        target = targets[slot]

        @pl.when(target >= 0)
        def _():
            out[target] = out[target] + got[slot]


def first_blocks(targets, got, start):
    vmem = pl.BlockSpec(memory_space=pltpu.VMEM)
    return pl.pallas_call(
        first_kernel,
        out_shape=jax.ShapeDtypeStruct(start.shape, jnp.float32),
        in_specs=[pl.BlockSpec(memory_space=pltpu.SMEM), vmem, vmem],
        out_specs=vmem,
        compiler_params=pltpu.CompilerParams(vmem_limit_bytes=VMEM_LIMIT),
        cost_estimate=pl.CostEstimate(
            flops=got.size, bytes_accessed=4 * (got.size + 2 * start.size), transcendentals=0
        ),
        name="first_blocks",
    )(targets, got, start)


def tables(every, n_row, n_col, capacity, order):
    row, col = lax.axis_index("row"), lax.axis_index("col")
    count = every.shape[-1]
    every = every.reshape(n_row, n_col, 2, count)
    places = jnp.arange(capacity, dtype=jnp.int32)
    columns = jnp.arange(n_col, dtype=jnp.int32)
    visits = jnp.asarray(order, jnp.int32)[row]

    def spread(match, values):
        rank = jnp.cumsum(match.astype(jnp.int32), axis=-1) - 1
        hit = match[..., None, :] & (rank[..., None, :] == places[:, None])
        return jnp.max(jnp.where(hit, values[..., None, :], -1), axis=-1)

    column = lax.dynamic_index_in_dim(every[:, :, 0], col, axis=1, keepdims=False)[visits]
    numbers = jnp.arange(count, dtype=jnp.int32)

    def slots_of(blocks, owners):
        match = blocks[:, None, :] == owners[..., None]
        return spread(match, jnp.broadcast_to(numbers, match.shape)).reshape(len(blocks), -1)

    def listed(sent):
        there = (sent >= 0).astype(jnp.int32)
        used = jnp.sum(there, axis=-1, keepdims=True)
        rank = jnp.cumsum(there, axis=-1)
        wanted = jnp.minimum(jnp.arange(sent.shape[-1], dtype=jnp.int32) + 1, used)
        full = jnp.argmax(rank[:, None, :] >= wanted[..., None], axis=-1).astype(jnp.int32)
        return sent, full, used

    sent = listed(slots_of(column[:-1], jnp.broadcast_to(row * n_col + columns, (n_row - 1, n_col))))
    beside = jnp.where(row == 1, 0, jnp.where(row == n_row - 2, n_row - 1, -1))
    inside = jnp.where((row == 0) | (row == n_row - 1), -1, row)
    rows = jnp.stack([inside, beside])
    owners = jnp.where(rows[:, None] >= 0, rows[:, None] * n_col + columns, -1)
    final = listed(slots_of(column[-1:], owners.reshape(1, -1)))

    arriving = every[visits]
    got = spread(arriving[:, :, 0] == row * n_col + col, arriving[:, :, 1])
    got = got.reshape(n_row, n_col * capacity)
    leader = jnp.argmax(got[:, :, None] == got[:, None, :], axis=-1).astype(jnp.int32)
    names = ("sent", "full", "used", "last sent", "last full", "last used", "got", "leader")
    return dict(zip(names, (*sent, *final, got, leader)))


def per_device(a_panels, b_panels, a_occupancy, b_occupancy, owner_device, owner_block, c_previous):
    n_row = lax.axis_size("row")
    n_col = lax.axis_size("col")
    row, col = lax.axis_index("row"), lax.axis_index("col")
    images = n_col // n_row
    inner = b_panels.shape[0] // images
    count_blocks = owner_block.size
    capacity = max(2, (2 * count_blocks + n_row * n_col - 1) // (n_row * n_col))
    order = visit_order(n_row)
    every_row = list(range(n_row))
    early = list(range(TICKS - 1))
    backward = [((c + 1) % n_col, c) for c in range(n_col)]

    def image(number, part):
        depth = inner // PARTS
        start = (row + col + number * n_row) % n_col // n_row * inner + part * depth
        present = lax.dynamic_slice_in_dim(b_occupancy, start // BLK, depth // BLK, 0)
        return widen(present, lax.dynamic_slice_in_dim(b_panels, start, depth, 0))

    held = {("A", 0, 0): widen(a_occupancy, a_panels)}
    for part in range(PARTS):
        held["Y", part, 0] = image(1, part)
        held["X", part, 0] = image(0, part)
    mine = jnp.stack([owner_device.reshape(-1), owner_block.reshape(-1)])
    held["owners"] = jnp.broadcast_to(mine, (n_row * n_col,) + mine.shape)

    reach = n_row - 1
    first = [(("A", 0, -d), ("A", 0, d)) for d in range(1, reach)]
    lower = [(("Y", part, -d), ("X", part, d)) for d in range(1, n_row) for part in range(PARTS)]
    steps = []
    for number in range(max(len(first), len(lower))):
        steps += first[number : number + 1] + lower[number : number + 1]
    for d in range(1, reach):
        steps += [(("C", part, -d), ("Y", part, d)) for part in range(PARTS)]
    steps = [((("C", key[1], 0), other) if key[::2] == ("Y", -reach) else (key, other)) for key, other in steps]
    ends = {keys[0]: number for number, keys in enumerate(steps)}

    def relay(key):
        kind, part, offset = key
        sources = early if kind == "Y" else every_row
        if kind == "C":
            lower = held.get(("C", part, offset + 1), held["X", part, 0])
            later = held.get(("C", part, offset + 2), held["X", part, 0])
            later = held["Y", part, 1 - reach] if offset == 0 else later
            pairs = [(r, r + 1) for r in range(n_row - 1) if r == reach - 1 or -offset < reach - 1]
            return lax.ppermute(jnp.where(row == reach - 1, later, lower), "row", pairs)
        if offset < 0:
            return up_step(held[kind, part, offset + 1], sources, -offset, n_row)
        if kind == "Y" and offset > TICKS - 3:
            return None
        return down_step(held[kind, part, offset - 1], sources, offset)

    def close(due):
        held.update(due)
        held.update(zip(list(held), lax.optimization_barrier(tuple(held.values()))))

    def hops(name, panels):
        found = {(name, 0): panels}
        for t in range(1, TICKS):
            found[name, t] = lax.ppermute(found[name, t - 1], "col", backward)
        return found

    def working(step):
        return [min(max(r, 1), n_row - 2) if step == n_row - 1 else r for r in range(n_row)]

    def chosen(step):
        offsets = [order[r][step] - r for r in working(step)]
        kinds = sorted(set(offsets))
        index = jnp.asarray([kinds.index(o) for o in offsets], jnp.int32)[row]
        cases = [held["A", 0, k] for k in kinds]
        return lax.select_n(index if len(cases) > 2 else index == 1, *cases)

    def product(step):
        keys = [
            [image_key(r, order[r][step] + t, n_row) for t in range(TICKS)] for r in working(step)
        ]
        names = sorted({key for of_row in keys for key in of_row})
        choices = [
            {t for r in range(n_row) for t in range(TICKS) if keys[r][t] == name} for name in names
        ]
        index = [[names.index(key) for key in of_row] for of_row in keys]
        which = jnp.asarray(index, jnp.int32)[row]
        last = step == n_row - 1
        of_step = ["last sent", "last full", "last used"] if last else ["sent", "full", "used"]
        return products(
            [held[name][0 if last else step] for name in of_step],
            which,
            [held["own" if step == 0 else "rest", t] for t in range(TICKS)],
            [[held[kind, part, offset] for part in range(PARTS)] for kind, offset in names],
            choices,
            max(step - 1, 0),
            4 if last else 1,
        )

    def exchange(step, blocks, total):
        targets, leader = held["got"][step], held["leader"][step]
        arrived = lax.all_to_all(blocks, "col", split_axis=0, concat_axis=0, tiled=True)
        if step == 0:
            return first_blocks(targets, arrived, total)
        return add_blocks(targets, leader, arrived, total)

    start_of = {ends["C", PARTS - 1, -step] + 2: step for step in range(reach)}
    last_number = ends["C", PARTS - 1, 2 - reach] + 2
    total = c_previous.reshape(c_previous.shape[2:])
    exchange_at = {at + (1 if step < reach - 2 else 2): step for at, step in start_of.items()}
    beside = [(1, 0), (n_row - 2, n_row - 1)]
    flying = {number: {} for number in range(2, 11)}
    for number in range(len(steps) + 2):
        if number >= 2:
            close(flying.pop(number, {}))
        if number == last_number + 1:
            flying[len(steps) + 2] = {"half": lax.ppermute(held["side", 2], "row", beside)}
        step = exchange_at.get(number)
        if step is not None:
            total = exchange(step, held["blocks", step], total)
        if number < len(steps):
            moving = {key: relay(key) for key in steps[number]}
            flying.setdefault(number + 2, {}).update(
                {key: value for key, value in moving.items() if value is not None}
            )
        if number == 0:
            flying[3].update(hops("own", held["A", 0, 0][None]))
        if number == ends["A", 0, 1 - reach] + 2:
            panels = jnp.stack([chosen(step) for step in range(1, n_row)])
            flying.setdefault(number + 7, {}).update(hops("rest", panels))
        if number == 2:
            every = lax.all_to_all(held["owners"], ("row", "col"), 0, 0, tiled=True)
            flying[5]["every"] = every
        if number == 5:
            flying[number + 1].update(tables(held["every"], n_row, n_col, capacity, order))
        if number in start_of and number < len(steps) + 1:
            (blocks,) = product(start_of[number])
            flying.setdefault(number + 1, {})["blocks", start_of[number]] = blocks
        if number == last_number:
            sides = product(n_row - 1)
            flying.setdefault(number + 1, {}).update({("side", k): v for k, v in enumerate(sides)})
    (blocks,) = product(n_row - 2)
    close({"blocks": blocks, **flying.pop(len(steps) + 2)})
    far = [held["half"], lax.ppermute(held["side", 3], "row", beside)]
    total = exchange(n_row - 2, held["blocks"], total)
    edge = (row == 0) | (row == n_row - 1)
    blocks = jnp.concatenate([jnp.where(edge, far[k], held["side", k]) for k in range(2)])
    total = exchange(n_row - 1, blocks, total)
    return total.reshape(c_previous.shape)


def solution(mesh):
    in_specs = (
        P("row", "col"),
        P("row", "col"),
        P("row", "col"),
        P("row", "col"),
        P("row", "col", None, None),
        P("row", "col", None),
        P("row", "col", None, None, None),
    )
    out_specs = P("row", "col", None, None, None)
    return jax.shard_map(
        per_device, mesh=mesh, in_specs=in_specs, out_specs=out_specs, check_vma=False
    )
```
